32 devices in a mesh: groups: 2 (over y), slab: 4 (over z), pole: 2 (over x), sub: 2 (over core).
Axes of the slice: x: 2, y: 2, z: 4, core: 2. Of those that a mesh axis runs over, the one named last changes fastest.
Arguments:
- onsite: float32 [8, 2, 128, 128], P(('groups', 'slab')), parts along dimension 0, may hold values from -0.5 to 0.5
- coupling: float32 [8, 2, 128, 128], P(('groups', 'slab')), parts along dimension 0, may hold values from -0.25 to 0.25
- pole_real: float32 [4], P(('pole', 'sub')), may hold values from -2 to 2
- pole_imag: float32 [4], P(('pole', 'sub')), may hold values from 0.1 to 1
- pole_weight: float32 [4, 2], P(('pole', 'sub')), may hold values from -4 to 4
Outputs:
- density: float32 [8, 2, 128, 128], P(('groups', 'slab'), None, ('pole', 'sub')), parts along dimension 0
- energy_density: float32 [8, 2, 128, 128], P(('groups', 'slab'), None, ('pole', 'sub')), parts along dimension 0
The draws below stay inside these ranges and needn't reach their ends.
There are 2 independent parts, one for each index of `groups`. The reference program is written for one: setup_inputs(seed, part) draws one part's arguments, and reference() takes and returns one part's arrays. A program takes and returns all parts, laid end to end along the dimension named above; an argument that names none is the same for every part. Nothing has to cross between parts.
All inputs are finite; a program needn't handle non-finite values.
Results may differ from the reference program's by a relative error of at most 0.0003.
Values sent between devices are 32-bit elements; how exact they have to be, the bound alone decides.
No kernel may reach another device: no remote copies, remote signals or barrier semaphores. Data moves between devices by JAX's collectives and lax.ppermute only.
A program may use at most 128 MiB of HBM per device.

```python
import math
import jax
import jax.numpy as jnp
from jax import lax

B = 128
NB = 4
POLES = 4


def shard_levels(own_key, extent, split, smallest, high):
    def one(position, parts):
        heights = jax.random.uniform(jax.random.fold_in(jax.random.fold_in(own_key, 6), position), (parts,), jnp.float32, smallest / len(split), high / len(split))
        return jnp.repeat(jnp.exp(heights), extent[position] // parts).reshape((-1,) + (1,) * (len(extent) - position - 1))

    level = one(*split[0])
    for cut in split[1:]:
        level = level * one(*cut)
    return level


def centred(stream_key, dims, deviation, limit, shards=(), held_as=jnp.bfloat16):
    gain = shard_levels(stream_key, dims, shards, -0.22, 0.18) if shards else 1.0
    values = jax.random.normal(stream_key, dims, jnp.float32) * deviation * gain
    return jnp.minimum(jnp.maximum(values, -limit), limit).astype(held_as)


def setup_inputs(seed: int = 0, part: int = 0) -> dict:
    key_of = jax.random.split(jax.random.key(seed), 6)
    own_keys = jax.random.split(jax.random.fold_in(key_of[5], part), 6)
    return {
        "onsite": centred(own_keys[0], (NB, 2, B, B), B ** -0.5, 0.5, ((0, 4),), jnp.float32),
        "coupling": centred(own_keys[1], (NB, 2, B, B), (4 * B) ** -0.5, 0.25, ((0, 4),), jnp.float32),
        "pole_real": jnp.clip(jax.random.uniform(key_of[2], (POLES,), jnp.float32, -2.0, 2.0) * shard_levels(key_of[2], (POLES,), ((0, 4),), -0.4, 0.0), -2.0, 2.0),
        "pole_imag": jnp.clip(jnp.exp(math.log(1.0) - 2.3025851 * jax.random.uniform(key_of[3], (POLES,), jnp.float32) ** shard_levels(key_of[3], (POLES,), ((0, 4),), -0.2, 0.2)), 0.1, 1.0),
        "pole_weight": centred(key_of[4], (POLES, 2), 1.0, 4.0, ((0, 4),), jnp.float32),
    }


precise = lax.Precision.HIGHEST

def complex_product(left_part, right_part):
    real_part = jnp.matmul(left_part[..., 0, :, :], right_part[..., 0, :, :], precision=precise) - jnp.matmul(left_part[..., 1, :, :], right_part[..., 1, :, :], precision=precise)
    imag_part = jnp.matmul(left_part[..., 0, :, :], right_part[..., 1, :, :], precision=precise) + jnp.matmul(left_part[..., 1, :, :], right_part[..., 0, :, :], precision=precise)
    return jnp.stack([real_part, imag_part], axis=-3)

def adjoint(matrix):
    return jnp.stack([jnp.swapaxes(matrix[..., 0, :, :], -1, -2), -jnp.swapaxes(matrix[..., 1, :, :], -1, -2)], axis=-3)

def hermitian(matrix):
    return 0.5 * (matrix + adjoint(matrix))

def invert(matrix):
    block_order = matrix.shape[-1]
    conjugate = adjoint(matrix)
    gram = complex_product(conjugate, matrix)
    upper_rows = jnp.concatenate([gram[0], -gram[1]], axis=1)
    lower_rows = jnp.concatenate([gram[1], gram[0]], axis=1)
    factor = jnp.linalg.cholesky(jnp.concatenate([upper_rows, lower_rows], axis=0))
    stacked = jnp.concatenate([conjugate[0], conjugate[1]], axis=0)
    halfway = lax.linalg.triangular_solve(factor, stacked, left_side=True, lower=True)
    solved = lax.linalg.triangular_solve(factor, halfway, left_side=True, lower=True, transpose_a=True)
    return jnp.stack([solved[:block_order], solved[block_order:]])

def forward_sweep(start_inverse, start_pivot, coupled, shifted):

    def advance(state_now, item_pair):
        link_block, own_block = item_pair
        pivot_block = own_block - complex_product(adjoint(link_block), complex_product(state_now[0], link_block))
        inverse = invert(pivot_block)
        return ((inverse, pivot_block), inverse)
    (_, last_pivot), inverses = lax.scan(advance, (start_inverse, start_pivot), (coupled, shifted))
    return (last_pivot, inverses)

def takahashi(last_green, inverses, outward, inward):

    def retreat(green_next, triple):
        left_green, out_factor, in_factor = triple
        green_now = left_green + complex_product(out_factor, complex_product(green_next, in_factor))
        return (green_now, green_now)
    _, earlier = lax.scan(retreat, last_green, (inverses[:-1], outward, inward), reverse=True)
    return jnp.concatenate([earlier, last_green[None]], axis=0)

def weighted_part(greens, weight_re, weight_im):
    real_part = weight_re * greens[:, 0] - weight_im * greens[:, 1]
    imag_part = weight_re * greens[:, 1] + weight_im * greens[:, 0]
    return jnp.stack([0.5 * (imag_part + jnp.swapaxes(imag_part, 1, 2)), 0.5 * (jnp.swapaxes(real_part, 1, 2) - real_part)], axis=1)

def reference(onsite, coupling, pole_real, pole_imag, pole_weight):
    total_blocks = onsite.shape[0]
    block_order = onsite.shape[-1]
    identity_block = jnp.eye(block_order, dtype=jnp.float32)
    zeros_block = jnp.zeros((block_order, block_order), jnp.float32)
    unit = jnp.stack([identity_block, zeros_block])
    link_mask = (jnp.arange(total_blocks) > 0).astype(jnp.float32)
    coupled = coupling * link_mask[:, None, None, None]
    onsite_herm = hermitian(onsite)

    def one_pole(sums, pole_data):
        shift_re, shift_im, weight_re, weight_im = pole_data
        shifted = onsite_herm - jnp.stack([shift_re * identity_block, shift_im * identity_block])
        _, inverses = forward_sweep(unit, unit, coupled, shifted)
        outward = complex_product(inverses[:-1], coupled[1:])
        inward = complex_product(adjoint(coupled[1:]), inverses[:-1])
        greens = takahashi(inverses[-1], inverses, outward, inward)
        energy_re = weight_re * shift_re - weight_im * shift_im
        energy_im = weight_re * shift_im + weight_im * shift_re
        return ((sums[0] + weighted_part(greens, weight_re, weight_im), sums[1] + weighted_part(greens, energy_re, energy_im)), None)
    start = jnp.zeros((total_blocks, 2, block_order, block_order), jnp.float32)
    (density, energy_density), _ = lax.scan(one_pole, (start, start), (pole_real, pole_imag, pole_weight[:, 0], pole_weight[:, 1]))
    return (density, energy_density)
```

```python
import functools

import jax
import jax.numpy as jnp
from jax import lax
from jax.experimental import pallas as pl
from jax.experimental.pallas import tpu as pltpu
from jax.sharding import PartitionSpec as P

ROWS = 8
precise = lax.Precision.HIGHEST
f32 = jnp.float32


def row_of(tile, k):
    return jnp.broadcast_to(tile[k : k + 1, :], tile.shape)


def lane_of(tile, k):
    return jnp.broadcast_to(tile[:, k : k + 1], tile.shape)


def sweep_panel(xr, xi, first, lane, subl):
    cols = [(lane_of(xr, first + j), lane_of(xi, first + j)) for j in range(ROWS)]
    for k in range(ROWS):
        tr, ti = cols[k]
        dr, di = row_of(tr, k), row_of(ti, k)
        scale = 1.0 / (dr * dr + di * di)
        rr, ri = dr * scale, -di * scale
        cr, ci = tr - (subl == k).astype(f32), ti
        for j in range(k + 1, ROWS):
            ar, ai = row_of(cols[j][0], k), row_of(cols[j][1], k)
            br, bi = ar * rr - ai * ri, ar * ri + ai * rr
            cols[j] = (cols[j][0] - (cr * br - ci * bi), cols[j][1] - (cr * bi + ci * br))
        ar, ai = row_of(xr, k) + (lane == first + k).astype(f32), row_of(xi, k)
        br, bi = ar * rr - ai * ri, ar * ri + ai * rr
        xr, xi = xr - (cr * br - ci * bi), xi - (cr * bi + ci * br)
    return xr, xi


def invert_into(src, dst):
    order = src.shape[-1]
    count = order // ROWS
    lane = lax.broadcasted_iota(jnp.int32, (ROWS, order), 1)
    subl = lax.broadcasted_iota(jnp.int32, (ROWS, order), 0)
    re = [src[0, ROWS * i : ROWS * i + ROWS, :] for i in range(count)]
    im = [src[1, ROWS * i : ROWS * i + ROWS, :] for i in range(count)]
    for p in range(count):
        first = ROWS * p
        xr, xi = sweep_panel(re[p], im[p], first, lane, subl)
        rows = [(row_of(xr, k), row_of(xi, k)) for k in range(ROWS)]
        inside = (lane >= first) & (lane < first + ROWS)
        for q in range(1, count):
            i = (p + q) % count
            ar, ai = re[i], im[i]
            nr, ni = jnp.where(inside, 0.0, ar), jnp.where(inside, 0.0, ai)
            for k in range(ROWS):
                cr, ci = lane_of(ar, first + k), lane_of(ai, first + k)
                ur, ui = rows[k]
                nr = nr - cr * ur + ci * ui
                ni = ni - cr * ui - ci * ur
            re[i], im[i] = nr, ni
        re[p], im[p] = xr, xi
    for i in range(count):
        dst[0, ROWS * i : ROWS * i + ROWS, :] = re[i]
        dst[1, ROWS * i : ROWS * i + ROWS, :] = im[i]


def dot(a, b):
    return lax.dot_general(a, b, (((1,), (0,)), ((), ())), precision=precise, preferred_element_type=f32)


def product(a, b):
    order = a[0].shape[0]
    whole = dot(jnp.concatenate(a, axis=0), jnp.concatenate(b, axis=1))
    real = whole[:order, :order] - whole[order:, order:]
    imag = whole[:order, order:] + whole[order:, :order]
    return real, imag


def adjoint(a):
    return a[0].T, -a[1].T


def pair(ref, *index):
    return ref[(*index, 0)], ref[(*index, 1)]


def kernel(
    slabs, poles, place, pole, onsite, coupling, *refs
):
    gathered, refs = refs[: 2 * (slabs - 1)], refs[2 * (slabs - 1) :]
    outs, (blocks, links, work, inverses, pivot, greens) = refs[:poles], refs[poles:]
    me, mine, sub = place[0], place[1], place[2]
    half = slabs // 2
    order = onsite.shape[-1]
    blocks[me] = onsite[0]
    links[me] = coupling[0]
    for k in range(1, slabs):
        source = lax.rem(me + slabs - k, slabs)
        for part, ref in ((sub, gathered[2 * k - 2]), (1 - sub, gathered[2 * k - 1])):
            blocks[source, part] = ref[0]
            links[source, part] = ref[1]

    eye = (
        lax.broadcasted_iota(jnp.int32, (order, order), 0)
        == lax.broadcasted_iota(jnp.int32, (order, order), 1)
    ).astype(f32)
    zr, zi = pole[0], pole[1]

    def shifted(j):
        real, imag = pair(blocks, j)
        return 0.5 * (real + real.T) - zr * eye, 0.5 * (imag - imag.T) - zi * eye

    left = me < half

    def where_block(slot, j):
        from_left = left == (slot == 0)
        return from_left, jnp.where(from_left, j, slabs - 1 - j), jnp.where(from_left, j, slabs - j)

    def link(from_left, index):
        real, imag = pair(links, index)
        return (
            jnp.where(from_left, real, real.T),
            jnp.where(from_left, imag, -imag.T),
        )

    def put(ref, value, *index):
        ref[(*index, 0)] = value[0]
        ref[(*index, 1)] = value[1]

    def minus(a, b):
        return a[0] - b[0], a[1] - b[1]

    def level(j, _):
        def side(slot, _):
            from_left, own, joint = where_block(slot, j)

            @pl.when(j < half)
            def _():
                put(work, shifted(own))

            @pl.when((j > 0) & (j < half))
            def _():
                k = link(from_left, joint)
                inner = product(pair(inverses, slot, j - 1), k)
                put(work, minus(pair(work), product(adjoint(k), inner)))

            @pl.when(j == half)
            def _():
                k = link(jnp.logical_not(left), half)
                k = adjoint(k)
                inner = product(k, pair(inverses, 1, half - 1))
                put(work, minus(pair(pivot), product(inner, adjoint(k))))

            @pl.when(slot == 0)
            def _():
                pivot[...] = work[...]

            invert_into(work, inverses.at[slot, j])
            return 0

        return lax.fori_loop(0, jnp.where(j == half, 1, 2), side, 0)

    lax.fori_loop(0, half + 1, level, 0)
    greens[...] = inverses[0, half]
    place_in_chain = jnp.where(left, me, slabs - 1 - me)

    def outward(step, _):
        j = half - 1 - step
        _, _, joint = where_block(0, j)
        k = link(left, joint)
        inverse = pair(inverses, 0, j - 1)
        out = product(inverse, k)
        back = product(adjoint(k), inverse)
        update = product(product(out, pair(greens)), back)
        put(greens, (inverse[0] + update[0], inverse[1] + update[1]))
        return 0

    lax.fori_loop(0, half - 1 - place_in_chain, outward, 0)

    gr, gi = pair(greens)
    wr, wi = pole[2], pole[3]
    rows = order // poles
    for slot, (ur, ui) in enumerate(((wr, wi), (wr * zr - wi * zi, wr * zi + wi * zr))):
        real, imag = ur * gr - ui * gi, ur * gi + ui * gr
        put(work, (0.5 * (imag + imag.T), 0.5 * (real.T - real)))
        for k in range(poles):
            start = pl.multiple_of((mine ^ k) * rows, rows)
            for part in range(2):
                outs[k][slot, part] = work[part, pl.ds(start, rows), :]


def shards(slabs, poles, onsite, coupling, pole_real, pole_imag, pole_weight):
    order = onsite.shape[-1]
    me, sub = lax.axis_index("slab"), lax.axis_index("sub")
    mine = lax.axis_index(("pole", "sub"))
    halves = jnp.stack(
        [
            lax.dynamic_index_in_dim(onsite[0], sub, 0, False),
            lax.dynamic_index_in_dim(coupling[0], sub, 0, False),
        ]
    )
    gathered = []
    for k in range(1, slabs):
        got = lax.ppermute(halves, "slab", [(i, (i + k) % slabs) for i in range(slabs)])
        gathered += [got, lax.ppermute(got, "sub", [(0, 1), (1, 0)])]
    place = jnp.stack([me, mine, sub]).astype(jnp.int32)
    pole = jnp.concatenate([pole_real, pole_imag, pole_weight[0]])
    vmem = pl.BlockSpec(memory_space=pltpu.VMEM)
    smem = pl.BlockSpec(memory_space=pltpu.SMEM)
    half = slabs // 2
    pieces = pl.pallas_call(
        functools.partial(kernel, slabs, poles),
        out_shape=[jax.ShapeDtypeStruct((2, 2, order // poles, order), f32)] * poles,
        in_specs=[smem, smem] + [vmem] * (2 + len(gathered)),
        out_specs=[vmem] * poles,
        scratch_shapes=[
            pltpu.VMEM((slabs, 2, order, order), f32),
            pltpu.VMEM((slabs, 2, order, order), f32),
            pltpu.VMEM((2, order, order), f32),
            pltpu.VMEM((2, half + 1, 2, order, order), f32),
            pltpu.VMEM((2, order, order), f32),
            pltpu.VMEM((2, order, order), f32),
        ],
        compiler_params=pltpu.CompilerParams(vmem_limit_bytes=40 << 20),
    )(place, pole, onsite, coupling, *gathered)
    total = pieces[0]
    for k in range(1, poles):
        total = total + lax.ppermute(pieces[k], ("pole", "sub"), [(i, i ^ k) for i in range(poles)])
    return total[0][None], total[1][None]


def solution(mesh):
    in_specs = (
        P(("groups", "slab"), None, None, None),
        P(("groups", "slab"), None, None, None),
        P(("pole", "sub")),
        P(("pole", "sub")),
        P(("pole", "sub"), None),
    )
    out_specs = (
        P(("groups", "slab"), None, ("pole", "sub"), None),
        P(("groups", "slab"), None, ("pole", "sub"), None),
    )
    body = functools.partial(shards, mesh.shape["slab"], mesh.shape["pole"] * mesh.shape["sub"])
    return jax.shard_map(body, mesh=mesh, in_specs=in_specs, out_specs=out_specs, check_vma=False)
```

```python
import functools

import jax
import jax.numpy as jnp
from jax import lax
from jax.experimental import pallas as pl
from jax.experimental.pallas import tpu as pltpu
from jax.sharding import PartitionSpec as P

ROWS = 8
PANEL = 2 * ROWS
f32, bf16 = jnp.float32, jnp.bfloat16
PARTS = ((0, 0), (0, 1), (1, 0), (1, 1), (0, 2), (2, 0))


def row_of(tile, k):
    return jnp.broadcast_to(tile[k : k + 1, :], tile.shape)


def lane_of(tile, k):
    where = jnp.full(tile.shape, k, jnp.int32)
    return jnp.take_along_axis(tile, where, axis=1, mode="promise_in_bounds")


def sweep(tiles, first, lane, subl):
    tiles = list(tiles)
    columns = [[(lane_of(xr, first + j), lane_of(xi, first + j)) for j in range(ROWS)] for xr, xi in tiles]
    for k in range(ROWS):
        in_row, in_lane = (subl == k).astype(f32), (lane == first + k).astype(f32)
        for s, cols in enumerate(columns):
            xr, xi = tiles[s]
            tr, ti = cols[k]
            dr, di = row_of(tr, k), row_of(ti, k)
            scale = 1.0 / (dr * dr + di * di)
            rr, ri = dr * scale, -di * scale
            cr = tr - in_row
            cr, ci = cr * rr - ti * ri, cr * ri + ti * rr
            for j in range(k + 1, ROWS):
                ar, ai = row_of(cols[j][0], k), row_of(cols[j][1], k)
                cols[j] = (cols[j][0] - (cr * ar - ci * ai), cols[j][1] - (cr * ai + ci * ar))
            ar, ai = row_of(xr, k) + in_lane, row_of(xi, k)
            tiles[s] = (xr - (cr * ar - ci * ai), xi - (cr * ai + ci * ar))
    return tiles


def follow(tile, swept, first, inside):
    ar, ai = tile
    nr, ni = jnp.where(inside, 0.0, ar), jnp.where(inside, 0.0, ai)
    pr = pi = None
    for k in range(ROWS):
        cr, ci = lane_of(ar, first + k), lane_of(ai, first + k)
        ur, ui = row_of(swept[0], k), row_of(swept[1], k)
        tr, ti = cr * ur - ci * ui, cr * ui + ci * ur
        if k % 2 == 0:
            nr, ni = nr - tr, ni - ti
        else:
            pr, pi = (tr, ti) if pr is None else (pr + tr, pi + ti)
    return nr - pr, ni - pi


def split(x):
    parts = [x.astype(bf16)]
    for _ in range(2):
        x = x - parts[-1].astype(f32)
        parts.append(x.astype(bf16))
    return parts


def times(left, right):
    columns = right[0].shape[1]
    lr, li = split(left[0]), split(left[1])
    rr, ri, rn = split(right[0]), split(right[1]), split(-right[1])
    lhs = jnp.concatenate([part for a, _ in PARTS for part in (lr[a], li[a])], axis=1)
    rhs = jnp.concatenate(
        [
            jnp.concatenate(pair, axis=1)
            for _, b in PARTS
            for pair in ((rr[b], ri[b]), (rn[b], rr[b]))
        ],
        axis=0,
    )
    whole = lax.dot_general(lhs, rhs, (((1,), (0,)), ((), ())), preferred_element_type=f32)
    return whole[:, :columns], whole[:, columns:]


def others_follow(tiles, panel, place):
    order = tiles[0][0].shape[1]

    def padded(part):
        rows = jnp.concatenate(part, axis=0)
        above = [jnp.zeros((PANEL * place, order), f32)] if place else []
        below = order - PANEL * (place + 1)
        return jnp.concatenate(above + [rows] + ([jnp.zeros((below, order), f32)] if below else []), axis=0)

    left = [jnp.concatenate(part, axis=0) for part in zip(*tiles)]
    right = [padded(part) for part in zip(*panel)]
    real, imag = times(left, right)
    return [(real[ROWS * t : ROWS * t + ROWS], imag[ROWS * t : ROWS * t + ROWS]) for t in range(len(tiles))]


def invert(systems):
    order = systems[0][0][0].shape[1]
    count, panels = order // ROWS, order // PANEL
    lane = lax.broadcasted_iota(jnp.int32, (ROWS, order), 1)
    subl = lax.broadcasted_iota(jnp.int32, (ROWS, order), 0)
    systems = [list(tiles) for tiles in systems]
    for place in range(panels):
        a, b = 2 * place, 2 * place + 1
        in_a = (lane >= ROWS * a) & (lane < ROWS * a + ROWS)
        in_b = (lane >= ROWS * b) & (lane < ROWS * b + ROWS)
        last = place == panels - 1
        ahead = (b + 1) % count
        first = sweep([tiles[a] for tiles in systems], ROWS * a, lane, subl)
        second = [follow(tiles[b], x, ROWS * a, in_a) for tiles, x in zip(systems, first)]
        if not last:
            soon = [follow(tiles[ahead], x, ROWS * a, in_a) for tiles, x in zip(systems, first)]
        second = sweep(second, ROWS * b, lane, subl)
        if not last:
            soon = [follow(tile, x, ROWS * b, in_b) for tile, x in zip(soon, second)]
        first = [follow(tile, x, ROWS * b, in_b) for tile, x in zip(first, second)]
        rest = [i for i in range(count) if i not in (a, b) and (last or i != ahead)]
        rest.sort(key=lambda i: (i - ahead) % count)
        for s, tiles in enumerate(systems):
            taken = rest + rest[-1:] if len(rest) % 2 else rest
            delta = others_follow([tiles[i] for i in taken], [first[s], second[s]], place)
            for (dr, di), i in zip(delta, rest):
                tiles[i] = (
                    jnp.where(in_a | in_b, 0.0, tiles[i][0]) - dr,
                    jnp.where(in_a | in_b, 0.0, tiles[i][1]) - di,
                )
            tiles[a], tiles[b] = first[s], second[s]
            if not last:
                tiles[ahead] = soon[s]
    return systems


def to_tiles(value):
    count = value[0].shape[0] // ROWS
    return [tuple(part[ROWS * i : ROWS * i + ROWS] for part in value) for i in range(count)]


def from_tiles(tiles):
    return tuple(jnp.concatenate(part, axis=0) for part in zip(*tiles))


def inverses_of(*values):
    return [from_tiles(tiles) for tiles in invert([to_tiles(value) for value in values])]


def adjoint(a):
    return a[0].T, -a[1].T


def plus(a, b):
    return a[0] + b[0], a[1] + b[1]


def minus(a, b):
    return a[0] - b[0], a[1] - b[1]


def get(ref, *index):
    return ref[(*index, 0)], ref[(*index, 1)]


def put(ref, value, *index):
    ref[(*index, 0)], ref[(*index, 1)] = value


def square(order):
    rows = lax.broadcasted_iota(jnp.int32, (order, order), 0)
    columns = lax.broadcasted_iota(jnp.int32, (order, order), 1)
    return rows, columns


def pack(onsite):
    real, imag = 0.5 * (onsite[0] + onsite[0].T), 0.5 * (onsite[1] - onsite[1].T)
    rows, columns = square(real.shape[0])
    return jnp.where(rows <= columns, real, imag)


def unpack_shifted(packed, zr, zi):
    rows, columns = square(packed.shape[0])
    turned = packed.T
    real = jnp.where(rows <= columns, packed, turned)
    imag = jnp.where(rows > columns, packed, -turned)
    return jnp.where(rows == columns, real - zr, real), jnp.where(rows == columns, -zi, imag)


def prepare(place, onsite, coupling, packed, half):
    packed[...] = pack((onsite[0, 0], onsite[0, 1]))
    half[...] = coupling[0, place[2]]


def start_chain(slabs, place, pole, *refs):
    blocks, out, chosen = refs[: slabs // 2], refs[-2], refs[-1]
    me = place[0]
    end = jnp.where(me < slabs // 2, 0, slabs - 1)
    for k, ref in enumerate(blocks):

        @pl.when((me ^ end) == k)
        def _(ref=ref):
            chosen[...] = ref[...]

    (inverse,) = inverses_of(unpack_shifted(chosen[...], pole[0], pole[1]))
    put(out, inverse)


def finish(slabs, poles, place, pole, start, coupling, *refs):
    packed, refs = refs[:slabs], refs[slabs:]
    halves, refs = refs[: 2 * (slabs - 1)], refs[2 * (slabs - 1) :]
    outs, (blocks, links, outward, inward, own, far, work, greens) = refs[:poles], refs[poles:]
    me, mine, sub = place[0], place[1], place[2]
    middle = slabs // 2
    order = start.shape[-1]
    for k in range(slabs):
        blocks[me ^ k] = packed[k][...]
    links[me] = coupling[0]
    for k in range(1, slabs):
        links[me ^ k, sub] = halves[2 * k - 2][...]
        links[me ^ k, 1 - sub] = halves[2 * k - 1][...]
    zr, zi = pole[0], pole[1]
    left = me < middle

    def block(from_left, j):
        return unpack_shifted(blocks[jnp.where(from_left, j, slabs - 1 - j)], zr, zi)

    def link(from_left, j):
        real, imag = get(links, jnp.where(from_left, j, slabs - j))
        return jnp.where(from_left, real, real.T), jnp.where(from_left, imag, -imag.T)

    def reduced(from_left, j, inverse):
        k = link(from_left, j)
        out, back = times(inverse, k), adjoint(k)
        return times(back, out), out, times(back, inverse)

    put(own, (start[0], start[1]), 0)
    right = jnp.logical_not(left)

    def level(j, far_pivot):
        taken, out, back = reduced(left, j, get(own, j - 1))
        put(outward, out, j)
        put(inward, back, j)
        here, there = inverses_of(minus(block(left, j), taken), far_pivot())
        put(own, here, j)
        put(far, there, j - 1)

    def far_pivot(j):
        return minus(block(right, j), reduced(right, j, get(far, j - 1))[0])

    level(1, lambda: block(right, 0))

    def next_level(j, _):
        level(j, lambda: far_pivot(j - 1))
        return 0

    lax.fori_loop(2, middle, next_level, 0)
    taken, out, back = reduced(left, middle, get(own, middle - 1))
    put(outward, out, middle)
    put(inward, back, middle)
    (green,) = inverses_of(minus(far_pivot(middle - 1), taken))
    put(greens, green)

    def retreat(step, _):
        j = middle - step
        update = times(times(get(outward, j), get(greens)), get(inward, j))
        put(greens, plus(get(own, j - 1), update))
        return 0

    lax.fori_loop(0, middle - jnp.where(left, me, slabs - 1 - me), retreat, 0)
    gr, gi = get(greens)
    wr, wi = pole[2], pole[3]
    rows = order // poles
    for slot, (ur, ui) in enumerate(((wr, wi), (wr * zr - wi * zi, wr * zi + wi * zr))):
        real, imag = ur * gr - ui * gi, ur * gi + ui * gr
        put(work, (0.5 * (imag + imag.T), 0.5 * (real.T - real)))
        for k in range(poles):
            begin = pl.multiple_of((mine ^ k) * rows, rows)
            for part in range(2):
                outs[k][slot, part] = work[part, pl.ds(begin, rows), :]


def shards(slabs, poles, onsite, coupling, pole_real, pole_imag, pole_weight):
    order = onsite.shape[-1]
    middle = slabs // 2
    place = jnp.stack(
        [lax.axis_index("slab"), lax.axis_index(("pole", "sub")), lax.axis_index("sub")]
    ).astype(jnp.int32)
    pole = jnp.concatenate([pole_real, pole_imag, pole_weight[0]])
    vmem = pl.BlockSpec(memory_space=pltpu.VMEM)
    smem = pl.BlockSpec(memory_space=pltpu.SMEM)
    params = pltpu.CompilerParams(vmem_limit_bytes=40 << 20)
    square_of = jax.ShapeDtypeStruct((order, order), f32)
    complex_of = jax.ShapeDtypeStruct((2, order, order), f32)

    def scratch(*lead):
        return pltpu.VMEM((*lead, order, order), f32)

    packed, half = pl.pallas_call(
        prepare,
        out_shape=[square_of, square_of],
        in_specs=[smem, vmem, vmem],
        out_specs=[vmem, vmem],
        compiler_params=params,
    )(place, onsite, coupling)

    def swap(value, k):
        return lax.ppermute(value, "slab", [(i, i ^ k) for i in range(slabs)])

    blocks = [packed] + [swap(packed, k) for k in range(1, slabs)]
    halves = []
    for k in range(1, slabs):
        got = swap(half, k)
        halves += [got, lax.ppermute(got, "sub", [(0, 1), (1, 0)])]
    start = pl.pallas_call(
        functools.partial(start_chain, slabs),
        out_shape=complex_of,
        in_specs=[smem, smem] + [vmem] * middle,
        out_specs=vmem,
        scratch_shapes=[scratch()],
        compiler_params=params,
        cost_estimate=pl.CostEstimate(flops=2 * 10**9, bytes_accessed=10**6, transcendentals=0),
    )(place, pole, *blocks[:middle])
    pieces = pl.pallas_call(
        functools.partial(finish, slabs, poles),
        out_shape=[jax.ShapeDtypeStruct((2, 2, order // poles, order), f32)] * poles,
        in_specs=[smem, smem] + [vmem] * (2 + slabs + len(halves)),
        out_specs=[vmem] * poles,
        scratch_shapes=[
            scratch(slabs),
            scratch(slabs, 2),
            scratch(middle + 1, 2),
            scratch(middle + 1, 2),
            scratch(middle, 2),
            scratch(middle, 2),
            scratch(2),
            scratch(2),
        ],
        compiler_params=params,
    )(place, pole, start, coupling, *blocks, *halves)
    total = pieces[0]
    for k in range(1, poles):
        total = total + lax.ppermute(pieces[k], ("pole", "sub"), [(i, i ^ k) for i in range(poles)])
    return total[0][None], total[1][None]


def solution(mesh):
    in_specs = (
        P(("groups", "slab"), None, None, None),
        P(("groups", "slab"), None, None, None),
        P(("pole", "sub")),
        P(("pole", "sub")),
        P(("pole", "sub"), None),
    )
    out_specs = (
        P(("groups", "slab"), None, ("pole", "sub"), None),
        P(("groups", "slab"), None, ("pole", "sub"), None),
    )
    body = functools.partial(shards, mesh.shape["slab"], mesh.shape["pole"] * mesh.shape["sub"])
    return jax.shard_map(body, mesh=mesh, in_specs=in_specs, out_specs=out_specs, check_vma=False)
```

```python
import functools

import jax
import jax.numpy as jnp
from jax import lax
from jax.experimental import pallas as pl
from jax.experimental.pallas import tpu as pltpu
from jax.sharding import PartitionSpec as P

ROWS = 8
PANEL = 2 * ROWS
f32, bf16 = jnp.float32, jnp.bfloat16
PARTS = ((0, 0), (0, 1), (1, 0), (1, 1), (0, 2), (2, 0))


def row_of(tile, k):
    return jnp.broadcast_to(tile[k : k + 1, :], tile.shape)


def lane_of(tile, k):
    where = jnp.full(tile.shape, k, jnp.int32)
    return jnp.take_along_axis(tile, where, axis=1, mode="promise_in_bounds")


def sweep(tiles, first, lane, subl):
    tiles = list(tiles)
    columns = [[(lane_of(xr, first + j), lane_of(xi, first + j)) for j in range(ROWS)] for xr, xi in tiles]
    for k in range(ROWS):
        in_row, in_lane = (subl == k).astype(f32), (lane == first + k).astype(f32)
        for s, cols in enumerate(columns):
            xr, xi = tiles[s]
            tr, ti = cols[k]
            dr, di = row_of(tr, k), row_of(ti, k)
            scale = 1.0 / (dr * dr + di * di)
            rr, ri = dr * scale, -di * scale
            cr = tr - in_row
            cr, ci = cr * rr - ti * ri, cr * ri + ti * rr
            for j in range(k + 1, ROWS):
                ar, ai = row_of(cols[j][0], k), row_of(cols[j][1], k)
                cols[j] = (cols[j][0] - (cr * ar - ci * ai), cols[j][1] - (cr * ai + ci * ar))
            ar, ai = row_of(xr, k) + in_lane, row_of(xi, k)
            tiles[s] = (xr - (cr * ar - ci * ai), xi - (cr * ai + ci * ar))
    return tiles


def follow(tile, swept, first, inside):
    ar, ai = tile
    nr, ni = jnp.where(inside, 0.0, ar), jnp.where(inside, 0.0, ai)
    pr = pi = None
    for k in range(ROWS):
        cr, ci = lane_of(ar, first + k), lane_of(ai, first + k)
        ur, ui = row_of(swept[0], k), row_of(swept[1], k)
        tr, ti = cr * ur - ci * ui, cr * ui + ci * ur
        if k % 2 == 0:
            nr, ni = nr - tr, ni - ti
        else:
            pr, pi = (tr, ti) if pr is None else (pr + tr, pi + ti)
    return nr - pr, ni - pi


def split(x):
    parts = [x.astype(bf16)]
    for _ in range(2):
        x = x - parts[-1].astype(f32)
        parts.append(x.astype(bf16))
    return parts


def times(left, right):
    columns = right[0].shape[1]
    lr, li = split(left[0]), split(left[1])
    rr, ri, rn = split(right[0]), split(right[1]), split(-right[1])
    lhs = jnp.concatenate([part for a, _ in PARTS for part in (lr[a], li[a])], axis=1)
    rhs = jnp.concatenate(
        [
            jnp.concatenate(pair, axis=1)
            for _, b in PARTS
            for pair in ((rr[b], ri[b]), (rn[b], rr[b]))
        ],
        axis=0,
    )
    whole = lax.dot_general(lhs, rhs, (((1,), (0,)), ((), ())), preferred_element_type=f32)
    return whole[:, :columns], whole[:, columns:]


def others_follow(tiles, panel, place):
    order = tiles[0][0].shape[1]

    def padded(part):
        rows = jnp.concatenate(part, axis=0)
        above = [jnp.zeros((PANEL * place, order), f32)] if place else []
        below = order - PANEL * (place + 1)
        return jnp.concatenate(above + [rows] + ([jnp.zeros((below, order), f32)] if below else []), axis=0)

    left = [jnp.concatenate(part, axis=0) for part in zip(*tiles)]
    right = [padded(part) for part in zip(*panel)]
    real, imag = times(left, right)
    return [(real[ROWS * t : ROWS * t + ROWS], imag[ROWS * t : ROWS * t + ROWS]) for t in range(len(tiles))]


def invert(systems):
    order = systems[0][0][0].shape[1]
    count, panels = order // ROWS, order // PANEL
    lane = lax.broadcasted_iota(jnp.int32, (ROWS, order), 1)
    subl = lax.broadcasted_iota(jnp.int32, (ROWS, order), 0)
    systems = [list(tiles) for tiles in systems]
    for place in range(panels):
        a, b = 2 * place, 2 * place + 1
        in_a = (lane >= ROWS * a) & (lane < ROWS * a + ROWS)
        in_b = (lane >= ROWS * b) & (lane < ROWS * b + ROWS)
        last = place == panels - 1
        ahead = (b + 1) % count
        first = sweep([tiles[a] for tiles in systems], ROWS * a, lane, subl)
        second = [follow(tiles[b], x, ROWS * a, in_a) for tiles, x in zip(systems, first)]
        if not last:
            soon = [follow(tiles[ahead], x, ROWS * a, in_a) for tiles, x in zip(systems, first)]
        second = sweep(second, ROWS * b, lane, subl)
        if not last:
            soon = [follow(tile, x, ROWS * b, in_b) for tile, x in zip(soon, second)]
        first = [follow(tile, x, ROWS * b, in_b) for tile, x in zip(first, second)]
        rest = [i for i in range(count) if i not in (a, b) and (last or i != ahead)]
        rest.sort(key=lambda i: (i - ahead) % count)
        for s, tiles in enumerate(systems):
            taken = rest + rest[-1:] if len(rest) % 2 else rest
            delta = others_follow([tiles[i] for i in taken], [first[s], second[s]], place)
            for (dr, di), i in zip(delta, rest):
                tiles[i] = (
                    jnp.where(in_a | in_b, 0.0, tiles[i][0]) - dr,
                    jnp.where(in_a | in_b, 0.0, tiles[i][1]) - di,
                )
            tiles[a], tiles[b] = first[s], second[s]
            if not last:
                tiles[ahead] = soon[s]
    return systems


def to_tiles(value):
    count = value[0].shape[0] // ROWS
    return [tuple(part[ROWS * i : ROWS * i + ROWS] for part in value) for i in range(count)]


def from_tiles(tiles):
    return tuple(jnp.concatenate(part, axis=0) for part in zip(*tiles))


def inverses_of(*values):
    return [from_tiles(tiles) for tiles in invert([to_tiles(value) for value in values])]


def adjoint(a):
    return a[0].T, -a[1].T


def plus(a, b):
    return a[0] + b[0], a[1] + b[1]


def minus(a, b):
    return a[0] - b[0], a[1] - b[1]


def get(ref, *index):
    return ref[(*index, 0)], ref[(*index, 1)]


def put(ref, value, *index):
    ref[(*index, 0)], ref[(*index, 1)] = value


def square(order):
    rows = lax.broadcasted_iota(jnp.int32, (order, order), 0)
    columns = lax.broadcasted_iota(jnp.int32, (order, order), 1)
    return rows, columns


def pack(onsite):
    real, imag = 0.5 * (onsite[0] + onsite[0].T), 0.5 * (onsite[1] - onsite[1].T)
    rows, columns = square(real.shape[0])
    return jnp.where(rows <= columns, real, imag)


def unpack_shifted(packed, zr, zi):
    rows, columns = square(packed.shape[0])
    turned = packed.T
    real = jnp.where(rows <= columns, packed, turned)
    imag = jnp.where(rows > columns, packed, -turned)
    return jnp.where(rows == columns, real - zr, real), jnp.where(rows == columns, -zi, imag)


def prepare(pole_real, pole_imag, pole_weight, onsite, packed, pole):
    packed[...] = pack((onsite[0, 0], onsite[0, 1]))
    scalars = (pole_real[0], pole_imag[0], pole_weight[0, 0], pole_weight[0, 1])
    for row, value in enumerate(scalars):
        pole[row : row + 1, :] = jnp.full((1, pole.shape[1]), value, f32)


def scalars_of(pole):
    return [pole[row : row + 1, :] for row in range(4)]


def chain_end(slabs, me):
    return jnp.where(me < slabs // 2, 0, slabs - 1)


def start_chain(slabs, pole, *refs):
    blocks, out, chosen = refs[: slabs // 2], refs[-2], refs[-1]
    me = lax.axis_index("slab")
    distance = me ^ chain_end(slabs, me)
    zr, zi, _, _ = scalars_of(pole)
    for k, ref in enumerate(blocks):

        @pl.when(distance == k)
        def _(ref=ref):
            chosen[...] = ref[...]

    (inverse,) = inverses_of(unpack_shifted(chosen[...], zr, zi))
    put(out, inverse)


def chain(slabs, left, blocks, links, zr, zi):
    def block(from_left, j):
        return unpack_shifted(blocks[jnp.where(from_left, j, slabs - 1 - j)], zr, zi)

    def link(from_left, j):
        real, imag = get(links, jnp.where(from_left, j, slabs - j))
        return jnp.where(from_left, real, real.T), jnp.where(from_left, imag, -imag.T)

    def reduced(from_left, j, inverse):
        k = link(from_left, j)
        out, back = times(inverse, k), adjoint(k)
        return times(back, out), out, times(back, inverse)

    return block, reduced


def advance(slabs, pole, start, *refs):
    packed, refs = refs[:slabs], refs[slabs:]
    near, (here, there, outward, inward, blocks, links) = refs[: slabs // 2], refs[slabs // 2 :]
    me = lax.axis_index("slab")
    left = me < slabs // 2
    zr, zi, _, _ = scalars_of(pole)
    for k in range(slabs):
        blocks[me ^ k] = packed[k][...]
    for k in range(slabs // 2):
        links[me ^ k] = near[k][0]
    block, reduced = chain(slabs, left, blocks, links, zr, zi)
    taken, out, back = reduced(left, 1, get(start))
    put(outward, out)
    put(inward, back)
    own, far = inverses_of(minus(block(left, 1), taken), block(jnp.logical_not(left), 0))
    put(here, own)
    put(there, far)


def finish(slabs, poles, pole, start, here, there, outward_1, inward_1, *refs):
    packed, couplings, refs = refs[:slabs], refs[slabs : 2 * slabs], refs[2 * slabs :]
    outs, (blocks, links, outward, inward, own, far, work, greens) = refs[:poles], refs[poles:]
    me, mine = lax.axis_index("slab"), lax.axis_index(("pole", "sub"))
    middle = slabs // 2
    order = start.shape[-1]
    for k in range(slabs):
        blocks[me ^ k] = packed[k][...]
        links[me ^ k] = couplings[k][0]
    zr, zi, wr, wi = scalars_of(pole)
    left = me < middle
    right = jnp.logical_not(left)
    block, reduced = chain(slabs, left, blocks, links, zr, zi)
    own[0], own[1], far[0] = start[...], here[...], there[...]
    outward[1], inward[1] = outward_1[...], inward_1[...]

    def far_pivot(j):
        return minus(block(right, j), reduced(right, j, get(far, j - 1))[0])

    def level(j, _):
        taken, out, back = reduced(left, j, get(own, j - 1))
        put(outward, out, j)
        put(inward, back, j)
        one, two = inverses_of(minus(block(left, j), taken), far_pivot(j - 1))
        put(own, one, j)
        put(far, two, j - 1)
        return 0

    if middle > 2:
        lax.fori_loop(2, middle, level, 0)
    taken, out, back = reduced(left, middle, get(own, middle - 1))
    put(outward, out, middle)
    put(inward, back, middle)
    (green,) = inverses_of(minus(far_pivot(middle - 1), taken))
    put(greens, green)

    def retreat(step, _):
        j = middle - step
        update = times(times(get(outward, j), get(greens)), get(inward, j))
        put(greens, plus(get(own, j - 1), update))
        return 0

    lax.fori_loop(0, middle - jnp.where(left, me, slabs - 1 - me), retreat, 0)
    gr, gi = get(greens)
    rows = order // poles
    for slot, (ur, ui) in enumerate(((wr, wi), (wr * zr - wi * zi, wr * zi + wi * zr))):
        real, imag = ur * gr - ui * gi, ur * gi + ui * gr
        put(work, (0.5 * (imag + imag.T), 0.5 * (real.T - real)))
        for k in range(poles):
            begin = pl.multiple_of((mine ^ k) * rows, rows)
            for part in range(2):
                outs[k][slot, part] = work[part, pl.ds(begin, rows), :]


def shards(slabs, poles, onsite, coupling, pole_real, pole_imag, pole_weight):
    order = onsite.shape[-1]
    middle = slabs // 2
    vmem = pl.BlockSpec(memory_space=pltpu.VMEM)
    smem = pl.BlockSpec(memory_space=pltpu.SMEM)
    params = pltpu.CompilerParams(vmem_limit_bytes=40 << 20)
    square_of = jax.ShapeDtypeStruct((order, order), f32)
    complex_of = jax.ShapeDtypeStruct((2, order, order), f32)

    def scratch(*lead):
        return pltpu.VMEM((*lead, order, order), f32)

    def cost(inversions):
        return pl.CostEstimate(
            flops=inversions * 25 * 10**8, bytes_accessed=inversions * 10**6, transcendentals=0
        )

    packed, pole = pl.pallas_call(
        prepare,
        out_shape=[square_of, jax.ShapeDtypeStruct((ROWS, order), f32)],
        in_specs=[smem, smem, smem, vmem],
        out_specs=[vmem, vmem],
        compiler_params=params,
    )(pole_real, pole_imag, pole_weight, onsite)

    def swap(value, k):
        return lax.ppermute(value, "slab", [(i, i ^ k) for i in range(slabs)])

    blocks = [packed] + [swap(packed, k) for k in range(1, slabs)]
    links = [coupling] + [swap(coupling, k) for k in range(1, slabs)]
    start = pl.pallas_call(
        functools.partial(start_chain, slabs),
        out_shape=complex_of,
        in_specs=[vmem] * (1 + middle),
        out_specs=vmem,
        scratch_shapes=[scratch()],
        compiler_params=params,
        cost_estimate=cost(2),
    )(pole, *blocks[:middle])
    second = pl.pallas_call(
        functools.partial(advance, slabs),
        out_shape=[complex_of] * 4,
        in_specs=[vmem] * (2 + slabs + middle),
        out_specs=[vmem] * 4,
        scratch_shapes=[scratch(slabs), scratch(slabs, 2)],
        compiler_params=params,
        cost_estimate=cost(2),
    )(pole, start, *blocks, *links[:middle])
    pieces = pl.pallas_call(
        functools.partial(finish, slabs, poles),
        out_shape=[jax.ShapeDtypeStruct((2, 2, order // poles, order), f32)] * poles,
        in_specs=[vmem] * (6 + 2 * slabs),
        out_specs=[vmem] * poles,
        scratch_shapes=[
            scratch(slabs),
            scratch(slabs, 2),
            scratch(middle + 1, 2),
            scratch(middle + 1, 2),
            scratch(middle, 2),
            scratch(middle, 2),
            scratch(2),
            scratch(2),
        ],
        compiler_params=params,
        cost_estimate=cost(2),
    )(pole, start, *second, *blocks, *links)
    total = pieces[0]
    for k in range(1, poles):
        total = total + lax.ppermute(pieces[k], ("pole", "sub"), [(i, i ^ k) for i in range(poles)])
    return total[0][None], total[1][None]


def solution(mesh):
    in_specs = (
        P(("groups", "slab"), None, None, None),
        P(("groups", "slab"), None, None, None),
        P(("pole", "sub")),
        P(("pole", "sub")),
        P(("pole", "sub"), None),
    )
    out_specs = (
        P(("groups", "slab"), None, ("pole", "sub"), None),
        P(("groups", "slab"), None, ("pole", "sub"), None),
    )
    body = functools.partial(shards, mesh.shape["slab"], mesh.shape["pole"] * mesh.shape["sub"])
    return jax.shard_map(body, mesh=mesh, in_specs=in_specs, out_specs=out_specs, check_vma=False)
```

```python
import functools

import jax
import jax.numpy as jnp
from jax import lax
from jax.experimental import pallas as pl
from jax.experimental.pallas import tpu as pltpu
from jax.sharding import PartitionSpec as P

ROWS = 8
PANEL = 2 * ROWS
f32, bf16 = jnp.float32, jnp.bfloat16
PARTS = ((0, 0), (0, 1), (1, 0), (1, 1), (0, 2), (2, 0))


def row_of(tile, k):
    return jnp.broadcast_to(tile[k : k + 1, :], tile.shape)


def lane_of(tile, k):
    where = jnp.full(tile.shape, k, jnp.int32)
    return jnp.take_along_axis(tile, where, axis=1, mode="promise_in_bounds")


def plus(a, b):
    return a[0] + b[0], a[1] + b[1]


def minus(a, b):
    return a[0] - b[0], a[1] - b[1]


def complex_times(a, b):
    return a[0] * b[0] - a[1] * b[1], a[0] * b[1] + a[1] * b[0]


def sweep_double(tiles, first, lane, subl):
    tiles = list(tiles)
    columns = [[(lane_of(xr, first + j), lane_of(xi, first + j)) for j in range(ROWS)] for xr, xi in tiles]
    for k in range(0, ROWS, 2):
        for s, cols in enumerate(columns):

            def entries(pair):
                return [(row_of(pair[0], i), row_of(pair[1], i)) for i in (k, k + 1)]

            (a, c), (b, d) = entries(cols[k]), entries(cols[k + 1])
            det = minus(complex_times(a, d), complex_times(b, c))
            scale = 1.0 / (det[0] * det[0] + det[1] * det[1])
            over = det[0] * scale, -det[1] * scale
            one = cols[k][0] - (subl == k).astype(f32), cols[k][1]
            two = cols[k + 1][0] - (subl == k + 1).astype(f32), cols[k + 1][1]
            one, two = (
                minus(complex_times(one, d), complex_times(two, c)),
                minus(complex_times(two, a), complex_times(one, b)),
            )
            for j in range(k + 2, min(k + 4, ROWS)):
                upper, lower = entries(cols[j])
                taken = plus(complex_times(one, upper), complex_times(two, lower))
                cols[j] = minus(cols[j], complex_times(taken, over))
            one, two = complex_times(one, over), complex_times(two, over)
            for j in range(k + 4, ROWS):
                upper, lower = entries(cols[j])
                cols[j] = minus(cols[j], plus(complex_times(one, upper), complex_times(two, lower)))
            upper, lower = entries(tiles[s])
            upper = upper[0] + (lane == first + k).astype(f32), upper[1]
            lower = lower[0] + (lane == first + k + 1).astype(f32), lower[1]
            tiles[s] = minus(tiles[s], plus(complex_times(one, upper), complex_times(two, lower)))
    return tiles


def sweep_single(tiles, first, lane, subl):
    tiles = list(tiles)
    columns = [[(lane_of(xr, first + j), lane_of(xi, first + j)) for j in range(ROWS)] for xr, xi in tiles]
    for k in range(ROWS):
        in_row, in_lane = (subl == k).astype(f32), (lane == first + k).astype(f32)
        for s, cols in enumerate(columns):
            xr, xi = tiles[s]
            tr, ti = cols[k]
            dr, di = row_of(tr, k), row_of(ti, k)
            scale = 1.0 / (dr * dr + di * di)
            rr, ri = dr * scale, -di * scale
            cr = tr - in_row
            cr, ci = cr * rr - ti * ri, cr * ri + ti * rr
            for j in range(k + 1, ROWS):
                ar, ai = row_of(cols[j][0], k), row_of(cols[j][1], k)
                cols[j] = (cols[j][0] - (cr * ar - ci * ai), cols[j][1] - (cr * ai + ci * ar))
            ar, ai = row_of(xr, k) + in_lane, row_of(xi, k)
            tiles[s] = (xr - (cr * ar - ci * ai), xi - (cr * ai + ci * ar))
    return tiles


def follow(tile, swept, first, inside):
    ar, ai = tile
    nr, ni = jnp.where(inside, 0.0, ar), jnp.where(inside, 0.0, ai)
    pr = pi = None
    for k in range(ROWS):
        cr, ci = lane_of(ar, first + k), lane_of(ai, first + k)
        ur, ui = row_of(swept[0], k), row_of(swept[1], k)
        tr, ti = cr * ur - ci * ui, cr * ui + ci * ur
        if k % 2 == 0:
            nr, ni = nr - tr, ni - ti
        else:
            pr, pi = (tr, ti) if pr is None else (pr + tr, pi + ti)
    return nr - pr, ni - pi


def split(x):
    parts = [x.astype(bf16)]
    for _ in range(2):
        x = x - parts[-1].astype(f32)
        parts.append(x.astype(bf16))
    return parts


def multiply(left, right, columns):
    lhs = jnp.concatenate([part for a, _ in PARTS for part in (left[0][a], left[1][a])], axis=1)
    rhs = jnp.concatenate(
        [
            jnp.concatenate(pair, axis=1)
            for _, b in PARTS
            for pair in ((right[0][b], right[1][b]), (-right[1][b], right[0][b]))
        ],
        axis=0,
    )
    whole = lax.dot_general(lhs, rhs, (((1,), (0,)), ((), ())), preferred_element_type=f32)
    return whole[:, :columns], whole[:, columns:]


def times(left, right):
    columns = right[0].shape[1]
    return multiply([split(part) for part in left], [split(part) for part in right], columns)


def others_follow(tiles, panel, place):
    order = tiles[0][0].shape[1]

    def padded(rows):
        above, below = PANEL * place, order - PANEL * (place + 1)
        parts = [jnp.zeros((above, order), bf16)] if above else []
        parts += [rows]
        parts += [jnp.zeros((below, order), bf16)] if below else []
        return jnp.concatenate(parts, axis=0)

    left = [split(jnp.concatenate(part, axis=0)) for part in zip(*tiles)]
    right = [[padded(rows) for rows in split(jnp.concatenate(part, axis=0))] for part in zip(*panel)]
    real, imag = multiply(left, right, order)
    return [(real[ROWS * t : ROWS * t + ROWS], imag[ROWS * t : ROWS * t + ROWS]) for t in range(len(tiles))]


def invert(systems):
    order = systems[0][0][0].shape[1]
    count, panels = order // ROWS, order // PANEL
    lane = lax.broadcasted_iota(jnp.int32, (ROWS, order), 1)
    subl = lax.broadcasted_iota(jnp.int32, (ROWS, order), 0)
    systems = [list(tiles) for tiles in systems]
    sweep = sweep_double if len(systems) == 1 else sweep_single
    for place in range(panels):
        a, b = 2 * place, 2 * place + 1
        in_a = (lane >= ROWS * a) & (lane < ROWS * a + ROWS)
        in_b = (lane >= ROWS * b) & (lane < ROWS * b + ROWS)
        soon = [] if place == panels - 1 else [b + 1, b + 2]
        first = sweep([tiles[a] for tiles in systems], ROWS * a, lane, subl)
        second = [follow(tiles[b], x, ROWS * a, in_a) for tiles, x in zip(systems, first)]
        ahead = [[follow(tiles[i], x, ROWS * a, in_a) for i in soon] for tiles, x in zip(systems, first)]
        second = sweep(second, ROWS * b, lane, subl)
        ahead = [[follow(tile, x, ROWS * b, in_b) for tile in pair] for pair, x in zip(ahead, second)]
        first = [follow(tile, x, ROWS * b, in_b) for tile, x in zip(first, second)]
        rest = [i for i in range(count) if i not in (a, b, *soon)]
        rest.sort(key=lambda i: (i - b) % count)
        for s, tiles in enumerate(systems):
            delta = others_follow([tiles[i] for i in rest], [first[s], second[s]], place)
            for (dr, di), i in zip(delta, rest):
                tiles[i] = (
                    jnp.where(in_a | in_b, 0.0, tiles[i][0]) - dr,
                    jnp.where(in_a | in_b, 0.0, tiles[i][1]) - di,
                )
            tiles[a], tiles[b] = first[s], second[s]
            for i, tile in zip(soon, ahead[s]):
                tiles[i] = tile
    return systems


def to_tiles(value):
    count = value[0].shape[0] // ROWS
    return [tuple(part[ROWS * i : ROWS * i + ROWS] for part in value) for i in range(count)]


def from_tiles(tiles):
    return tuple(jnp.concatenate(part, axis=0) for part in zip(*tiles))


def inverses_of(*values):
    return [from_tiles(tiles) for tiles in invert([to_tiles(value) for value in values])]


def adjoint(a):
    return a[0].T, -a[1].T


def get(ref, *index):
    return ref[(*index, 0)], ref[(*index, 1)]


def put(ref, value, *index):
    ref[(*index, 0)], ref[(*index, 1)] = value


def square(order):
    rows = lax.broadcasted_iota(jnp.int32, (order, order), 0)
    columns = lax.broadcasted_iota(jnp.int32, (order, order), 1)
    return rows, columns


def hermitian(onsite):
    return 0.5 * (onsite[0] + onsite[0].T), 0.5 * (onsite[1] - onsite[1].T)


def pack(block):
    rows, columns = square(block[0].shape[0])
    return jnp.where(rows <= columns, *block)


def unpack(packed):
    rows, columns = square(packed.shape[0])
    turned = packed.T
    imag = jnp.where(rows > columns, packed, jnp.where(rows < columns, -turned, 0.0))
    return jnp.where(rows <= columns, packed, turned), imag


def shifted(block, zr, zi):
    rows, columns = square(block[0].shape[0])
    return jnp.where(rows == columns, block[0] - zr, block[0]), jnp.where(rows == columns, -zi, block[1])


def prepare(onsite, packed):
    packed[...] = pack(hermitian(get(onsite, 0)))


def spread_scalars(pole_real, pole_imag, pole_weight, pole):
    width = pole.shape[1]
    pole[0:1, :] = jnp.broadcast_to(pole_real[...].reshape(1, 1), (1, width))
    pole[1:2, :] = jnp.broadcast_to(pole_imag[...].reshape(1, 1), (1, width))
    pole[2:3, :] = jnp.broadcast_to(pole_weight[:, 0:1], (1, width))
    pole[3:4, :] = jnp.broadcast_to(pole_weight[:, 1:2], (1, width))


def scalars_of(pole):
    return [pole[row : row + 1, :] for row in range(4)]


def turned_if(turn, value):
    return jnp.where(turn, value[0].T, value[0]), jnp.where(turn, -value[1].T, value[1])


def start_chain(slabs, pole, *refs):
    near, out, chosen = refs[: slabs // 2], refs[-2], refs[-1]
    me = lax.axis_index("slab")
    distance = me ^ jnp.where(me < slabs // 2, 0, slabs - 1)
    zr, zi, _, _ = scalars_of(pole)
    for k, ref in enumerate(near):

        @pl.when(distance == k)
        def _(ref=ref):
            chosen[...] = ref[...]

    (inverse,) = inverses_of(shifted(unpack(chosen[...]), zr, zi))
    put(out, inverse)


def chain(slabs, me, blocks, links, zr, zi):
    left = me < slabs // 2

    def block(own, j):
        index = jnp.where(left == own, j, slabs - 1 - j)
        return shifted(unpack(blocks[index]), zr, zi)

    def reduced(own, j, inverse):
        from_left = left == own
        k = turned_if(jnp.logical_not(from_left), get(links, jnp.where(from_left, j, slabs - j)))
        out, back = times(inverse, k), adjoint(k)
        return times(back, out), out, back

    return block, reduced


def fill_near(me, target, refs):
    for k, ref in enumerate(refs):
        target[me ^ k] = ref[...] if ref.ndim == target.ndim - 1 else ref[0]


def fill_far(me, target, refs):
    middle, core = target.shape[0] // 2, lax.axis_index("sub")
    for i, ref in enumerate(refs):
        mask = middle + i - i % 2 + jnp.where(i % 2 == 0, core, 1 - core)
        target[me ^ mask] = ref[...] if ref.ndim == target.ndim - 1 else ref[0]


def advance(slabs, pole, start, *refs):
    middle = slabs // 2
    block_refs, link_refs, refs = refs[:slabs], refs[slabs : slabs + middle], refs[slabs + middle :]
    here, there, outward, inward, blocks, links = refs
    me = lax.axis_index("slab")
    zr, zi, _, _ = scalars_of(pole)
    fill_near(me, blocks, block_refs[:middle])
    fill_far(me, blocks, block_refs[middle:])
    fill_near(me, links, link_refs)
    block, reduced = chain(slabs, me, blocks, links, zr, zi)
    inverse = get(start)
    taken, out, back = reduced(True, 1, inverse)
    put(outward, out)
    put(inward, times(back, inverse))
    own, other = inverses_of(minus(block(True, 1), taken), block(False, 0))
    put(here, own)
    put(there, other)


def finish(slabs, poles, pole, start, second, end, outward_1, inward_1, *refs):
    middle = slabs // 2
    block_refs, link_refs, refs = refs[:slabs], refs[slabs : 2 * slabs], refs[2 * slabs :]
    outs, (blocks, links, outward, inward, own, other, work) = refs[:poles], refs[poles:]
    me, mine = lax.axis_index("slab"), lax.axis_index(("pole", "sub"))
    order = start.shape[-1]
    fill_near(me, blocks, block_refs[:middle])
    fill_far(me, blocks, block_refs[middle:])
    fill_near(me, links, link_refs[:middle])
    fill_far(me, links, link_refs[middle:])
    zr, zi, wr, wi = scalars_of(pole)
    block, reduced = chain(slabs, me, blocks, links, zr, zi)
    own[0], own[1], other[0] = start[...], second[...], end[...]
    outward[1], inward[1] = outward_1[...], inward_1[...]

    def other_pivot(j):
        return minus(block(False, j), reduced(False, j, get(other, j - 1))[0])

    def level(j, _):
        inverse = get(own, j - 1)
        taken, out, back = reduced(True, j, inverse)
        one, two = inverses_of(minus(block(True, j), taken), other_pivot(j - 1))
        put(outward, out, j)
        put(inward, times(back, inverse), j)
        put(own, one, j)
        put(other, two, j - 1)
        return 0

    def wider(j, found):
        base, out, back = found
        near_out, near_back = get(outward, j), get(inward, j)
        base = plus(get(own, j - 1), times(times(near_out, base), near_back))
        return base, times(near_out, out), times(back, near_back)

    if middle > 2:
        lax.fori_loop(2, middle, level, 0)
    inverse = get(own, middle - 1)
    taken, out, back = reduced(True, middle, inverse)
    steps = middle - 1 - jnp.where(me < middle, me, slabs - 1 - me)
    found = inverse, out, times(back, inverse)
    if middle == 2:
        further = wider(1, found)
        found = jax.tree.map(lambda new, old: jnp.where(steps > 0, new, old), further, found)
    else:
        found = lax.fori_loop(0, steps, lambda step, found: wider(middle - 1 - step, found), found)
    (green,) = inverses_of(minus(other_pivot(middle - 1), taken))
    gr, gi = plus(found[0], times(times(found[1], green), found[2]))
    gr_t, gi_t = gr.T, gi.T
    even, odd = (0.5 * (gr + gr_t), 0.5 * (gi + gi_t)), (0.5 * (gr_t - gr), 0.5 * (gi_t - gi))
    rows = order // poles
    for slot, (ur, ui) in enumerate(((wr, wi), (wr * zr - wi * zi, wr * zi + wi * zr))):
        put(work, (ur * even[1] + ui * even[0], ur * odd[0] - ui * odd[1]), slot)
    for k in range(poles):
        begin = pl.multiple_of((mine ^ k) * rows, rows)
        outs[k][...] = work[:, :, pl.ds(begin, rows), :]


def shards(slabs, poles, onsite, coupling, pole_real, pole_imag, pole_weight):
    order = onsite.shape[-1]
    middle = slabs // 2
    vmem = pl.BlockSpec(memory_space=pltpu.VMEM)
    params = pltpu.CompilerParams(vmem_limit_bytes=40 << 20)
    square_of = jax.ShapeDtypeStruct((order, order), f32)
    complex_of = jax.ShapeDtypeStruct((2, order, order), f32)

    def scratch(*lead):
        return pltpu.VMEM((*lead, order, order), f32)

    def cost(inversions):
        return pl.CostEstimate(
            flops=inversions * 25 * 10**8, bytes_accessed=inversions * 10**6, transcendentals=0
        )

    def swap(value, k):
        return lax.ppermute(value, "slab", [(i, i ^ k) for i in range(slabs)])

    packed = pl.pallas_call(
        prepare, out_shape=square_of, in_specs=[vmem], out_specs=vmem, compiler_params=params
    )(onsite)
    pole = pl.pallas_call(
        spread_scalars,
        out_shape=jax.ShapeDtypeStruct((ROWS, order), f32),
        in_specs=[vmem] * 3,
        out_specs=vmem,
        compiler_params=params,
    )(pole_real, pole_imag, pole_weight)

    def far_swap(value, k):
        pairs = [(2 * i + c, 2 * (i ^ (k + c)) + c) for i in range(slabs) for c in range(2)]
        return lax.ppermute(value, ("slab", "sub"), pairs)

    near_blocks = [packed] + [swap(packed, k) for k in range(1, middle)]
    far_blocks = [far_swap(packed, k) for k in range(middle, slabs, 2)]
    near_links = [coupling] + [swap(coupling, k) for k in range(1, middle)]
    far_links = [far_swap(coupling, k) for k in range(middle, slabs, 2)]
    start = pl.pallas_call(
        functools.partial(start_chain, slabs),
        out_shape=complex_of,
        in_specs=[vmem] * (1 + middle),
        out_specs=vmem,
        scratch_shapes=[scratch()],
        compiler_params=params,
        cost_estimate=cost(2),
    )(pole, *near_blocks)

    def both(values):
        pairs = []
        for value in values:
            mine, _ = lax.optimization_barrier((value, start))
            pairs += [value, lax.ppermute(mine, "sub", [(0, 1), (1, 0)])]
        return pairs

    blocks, links = near_blocks + both(far_blocks), near_links + both(far_links)
    second = pl.pallas_call(
        functools.partial(advance, slabs),
        out_shape=[complex_of] * 4,
        in_specs=[vmem] * (2 + slabs + middle),
        out_specs=[vmem] * 4,
        scratch_shapes=[scratch(slabs), scratch(slabs, 2)],
        compiler_params=params,
        cost_estimate=cost(2),
    )(pole, start, *blocks, *near_links)
    pieces = pl.pallas_call(
        functools.partial(finish, slabs, poles),
        out_shape=[jax.ShapeDtypeStruct((2, 2, order // poles, order), f32)] * poles,
        in_specs=[vmem] * (6 + 2 * slabs),
        out_specs=[vmem] * poles,
        scratch_shapes=[
            scratch(slabs),
            scratch(slabs, 2),
            scratch(middle + 1, 2),
            scratch(middle + 1, 2),
            scratch(middle, 2),
            scratch(middle, 2),
            scratch(2, 2),
        ],
        compiler_params=params,
        cost_estimate=cost(2),
    )(pole, start, *second, *blocks, *links)
    total = pieces[0]
    for k in range(1, poles):
        total = total + lax.ppermute(pieces[k], ("pole", "sub"), [(i, i ^ k) for i in range(poles)])
    return total[0][None], total[1][None]


def solution(mesh):
    in_specs = (
        P(("groups", "slab"), None, None, None),
        P(("groups", "slab"), None, None, None),
        P(("pole", "sub")),
        P(("pole", "sub")),
        P(("pole", "sub"), None),
    )
    out_specs = (
        P(("groups", "slab"), None, ("pole", "sub"), None),
        P(("groups", "slab"), None, ("pole", "sub"), None),
    )
    body = functools.partial(shards, mesh.shape["slab"], mesh.shape["pole"] * mesh.shape["sub"])
    return jax.shard_map(body, mesh=mesh, in_specs=in_specs, out_specs=out_specs, check_vma=False)
```

```python
import functools

import jax
import jax.numpy as jnp
from jax import lax
from jax.experimental import pallas as pl
from jax.experimental.pallas import tpu as pltpu
from jax.sharding import PartitionSpec as P

ROWS = 8
PANEL = 2 * ROWS
f32, bf16 = jnp.float32, jnp.bfloat16
PARTS = ((0, 0), (1, 0), (0, 1), (1, 1), (0, 2), (2, 0))


def row_of(tile, k):
    return jnp.broadcast_to(tile[k : k + 1, :], tile.shape)


def lane_of(tile, k):
    where = jnp.full(tile.shape, k, jnp.int32)
    return jnp.take_along_axis(tile, where, axis=1, mode="promise_in_bounds")


def plus(a, b):
    return a[0] + b[0], a[1] + b[1]


def minus(a, b):
    return a[0] - b[0], a[1] - b[1]


def complex_times(a, b):
    return a[0] * b[0] - a[1] * b[1], a[0] * b[1] + a[1] * b[0]


def sweep_double(tiles, columns, first, lane, subl):
    tiles = list(tiles)
    columns = [list(cols) for cols in columns]
    for k in range(0, ROWS, 2):
        for s, cols in enumerate(columns):

            def entries(pair):
                return [(row_of(pair[0], i), row_of(pair[1], i)) for i in (k, k + 1)]

            (a, c), (b, d) = entries(cols[k]), entries(cols[k + 1])
            det = minus(complex_times(a, d), complex_times(b, c))
            scale = 1.0 / (det[0] * det[0] + det[1] * det[1])
            over = det[0] * scale, -det[1] * scale
            one = cols[k][0] - (subl == k).astype(f32), cols[k][1]
            two = cols[k + 1][0] - (subl == k + 1).astype(f32), cols[k + 1][1]
            one, two = (
                minus(complex_times(one, d), complex_times(two, c)),
                minus(complex_times(two, a), complex_times(one, b)),
            )
            for j in range(k + 2, min(k + 4, ROWS)):
                upper, lower = entries(cols[j])
                taken = plus(complex_times(one, upper), complex_times(two, lower))
                cols[j] = minus(cols[j], complex_times(taken, over))
            one, two = complex_times(one, over), complex_times(two, over)
            for j in range(k + 4, ROWS):
                upper, lower = entries(cols[j])
                cols[j] = minus(cols[j], plus(complex_times(one, upper), complex_times(two, lower)))
            upper, lower = entries(tiles[s])
            upper = upper[0] + (lane == first + k).astype(f32), upper[1]
            lower = lower[0] + (lane == first + k + 1).astype(f32), lower[1]
            tiles[s] = minus(tiles[s], plus(complex_times(one, upper), complex_times(two, lower)))
    return tiles


def sweep_single(tiles, columns, first, lane, subl):
    tiles = list(tiles)
    columns = [list(cols) for cols in columns]
    for k in range(ROWS):
        in_row, in_lane = (subl == k).astype(f32), (lane == first + k).astype(f32)
        for s, cols in enumerate(columns):
            xr, xi = tiles[s]
            tr, ti = cols[k]
            dr, di = row_of(tr, k), row_of(ti, k)
            scale = 1.0 / (dr * dr + di * di)
            rr, ri = dr * scale, -di * scale
            cr = tr - in_row
            cr, ci = cr * rr - ti * ri, cr * ri + ti * rr
            for j in range(k + 1, ROWS):
                ar, ai = row_of(cols[j][0], k), row_of(cols[j][1], k)
                cols[j] = (cols[j][0] - (cr * ar - ci * ai), cols[j][1] - (cr * ai + ci * ar))
            ar, ai = row_of(xr, k) + in_lane, row_of(xi, k)
            tiles[s] = (xr - (cr * ar - ci * ai), xi - (cr * ai + ci * ar))
    return tiles


def spread(tiles, first):
    return [
        [(lane_of(xr, first + k), lane_of(xi, first + k)) for k in range(ROWS)] for xr, xi in tiles
    ]


def follow(tile, columns, swept, inside):
    nr, ni = jnp.where(inside, 0.0, tile[0]), jnp.where(inside, 0.0, tile[1])
    pr = pi = None
    for k, column in enumerate(columns):
        tr, ti = complex_times(column, (row_of(swept[0], k), row_of(swept[1], k)))
        if k % 2 == 0:
            nr, ni = nr - tr, ni - ti
        else:
            pr, pi = (tr, ti) if pr is None else (pr + tr, pi + ti)
    return nr - pr, ni - pi


def follow_all(tiles, columns, swept, inside, after=None):
    if after is None or len(tiles) > 1:
        masks = [inside] * len(tiles)
    else:
        masks = [inside & (tile[1] == tile[1]) for tile in after]
    return [follow(*args) for args in zip(tiles, columns, swept, masks)]


def split(x):
    parts = [x.astype(bf16)]
    for _ in range(2):
        x = x - parts[-1].astype(f32)
        parts.append(x.astype(bf16))
    return parts


def multiply(left, right, columns):
    rows = left[0][0].shape[0]
    lhs = jnp.concatenate(
        [jnp.concatenate((left[0][a], left[1][a]), axis=0) for a, _ in PARTS], axis=1
    )
    rhs = jnp.concatenate(
        [jnp.concatenate((right[0][b], right[1][b]), axis=1) for _, b in PARTS], axis=0
    )
    whole = lax.dot_general(lhs, rhs, (((1,), (0,)), ((), ())), preferred_element_type=f32)
    return (
        whole[:rows, :columns] - whole[rows:, columns:],
        whole[:rows, columns:] + whole[rows:, :columns],
    )


def times(left, right):
    columns = right[0].shape[1]
    return multiply([split(part) for part in left], [split(part) for part in right], columns)


def others_follow(tiles, panel, place):
    order = tiles[0][0].shape[1]

    def padded(rows):
        above, below = PANEL * place, order - PANEL * (place + 1)
        parts = [jnp.zeros((above, order), bf16)] if above else []
        parts += [rows]
        parts += [jnp.zeros((below, order), bf16)] if below else []
        return jnp.concatenate(parts, axis=0)

    left = [split(jnp.concatenate(part, axis=0)) for part in zip(*tiles)]
    right = [[padded(rows) for rows in split(jnp.concatenate(part, axis=0))] for part in zip(*panel)]
    real, imag = multiply(left, right, order)
    return [(real[ROWS * t : ROWS * t + ROWS], imag[ROWS * t : ROWS * t + ROWS]) for t in range(len(tiles))]


def invert(systems, asides):
    order = systems[0][0][0].shape[1]
    count, panels = order // ROWS, order // PANEL
    lane = lax.broadcasted_iota(jnp.int32, (ROWS, order), 1)
    subl = lax.broadcasted_iota(jnp.int32, (ROWS, order), 0)
    systems = [list(tiles) for tiles in systems]
    sweep = sweep_double if len(systems) == 1 else sweep_single
    for place in range(panels):
        a, b = 2 * place, 2 * place + 1
        in_a = (lane >= ROWS * a) & (lane < ROWS * a + ROWS)
        in_b = (lane >= ROWS * b) & (lane < ROWS * b + ROWS)
        soon = [] if place == panels - 1 else [b + 1, b + 2]
        nexts = [[tiles[i] for tiles in systems] for i in soon]
        second = [tiles[b] for tiles in systems]
        if place == 0:
            columns = spread([tiles[a] for tiles in systems], ROWS * a)
        second_columns = spread(second, ROWS * a)
        next_columns = [spread(tiles, ROWS * a) for tiles in nexts]
        first = sweep([tiles[a] for tiles in systems], columns, ROWS * a, lane, subl)
        second = follow_all(second, second_columns, first, in_a)
        columns = spread(second, ROWS * b)
        nexts = [follow_all(tiles, cols, first, in_a, second) for tiles, cols in zip(nexts, next_columns)]
        next_columns = [spread(tiles, ROWS * b) for tiles in nexts]
        first_columns = spread(first, ROWS * b)
        second = sweep(second, columns, ROWS * b, lane, subl)
        for i, cols in enumerate(next_columns):
            nexts[i] = follow_all(nexts[i], cols, second, in_b, nexts[0] if i else None)
            if i == 0:
                columns = spread(nexts[0], ROWS * (b + 1))
        first = follow_all(first, first_columns, second, in_b, nexts[0] if nexts else None)
        rest = [i for i in range(count) if i not in (a, b, *soon)]
        rest.sort(key=lambda i: (i - b) % count)
        for s, tiles in enumerate(systems):
            delta = others_follow([tiles[i] for i in rest], [first[s], second[s]], place)
            for (dr, di), i in zip(delta, rest):
                tiles[i] = (
                    jnp.where(in_a | in_b, 0.0, tiles[i][0]) - dr,
                    jnp.where(in_a | in_b, 0.0, tiles[i][1]) - di,
                )
            tiles[a], tiles[b] = first[s], second[s]
            for i, tile in zip(soon, nexts):
                tiles[i] = tile[s]
        if place < len(asides):
            asides[place]()
    return systems


def to_tiles(value):
    count = value[0].shape[0] // ROWS
    return [tuple(part[ROWS * i : ROWS * i + ROWS] for part in value) for i in range(count)]


def from_tiles(tiles):
    return tuple(jnp.concatenate(part, axis=0) for part in zip(*tiles))


def inverses_of(*values, asides=()):
    return [from_tiles(tiles) for tiles in invert([to_tiles(value) for value in values], asides)]


def adjoint(a):
    return a[0].T, -a[1].T


def get(ref, *index):
    return ref[(*index, 0)], ref[(*index, 1)]


def put(ref, value, *index):
    ref[(*index, 0)], ref[(*index, 1)] = value


def square(order):
    rows = lax.broadcasted_iota(jnp.int32, (order, order), 0)
    columns = lax.broadcasted_iota(jnp.int32, (order, order), 1)
    return rows, columns


def hermitian(onsite):
    return 0.5 * (onsite[0] + onsite[0].T), 0.5 * (onsite[1] - onsite[1].T)


def pack(block):
    rows, columns = square(block[0].shape[0])
    return jnp.where(rows <= columns, *block)


def unpack(packed):
    rows, columns = square(packed.shape[0])
    turned = packed.T
    imag = jnp.where(rows > columns, packed, jnp.where(rows < columns, -turned, 0.0))
    return jnp.where(rows <= columns, packed, turned), imag


def shifted(block, zr, zi):
    rows, columns = square(block[0].shape[0])
    return jnp.where(rows == columns, block[0] - zr, block[0]), jnp.where(rows == columns, -zi, block[1])


def prepare(onsite, packed):
    packed[...] = pack(hermitian(get(onsite, 0)))


def spread_scalars(pole_real, pole_imag, pole_weight, pole):
    width = pole.shape[1]
    pole[0:1, :] = jnp.broadcast_to(pole_real[...].reshape(1, 1), (1, width))
    pole[1:2, :] = jnp.broadcast_to(pole_imag[...].reshape(1, 1), (1, width))
    pole[2:3, :] = jnp.broadcast_to(pole_weight[:, 0:1], (1, width))
    pole[3:4, :] = jnp.broadcast_to(pole_weight[:, 1:2], (1, width))


def scalars_of(pole):
    return [pole[row : row + 1, :] for row in range(4)]


def turned_if(turn, value):
    return jnp.where(turn, value[0].T, value[0]), jnp.where(turn, -value[1].T, value[1])


def start_chain(slabs, pole, *refs):
    near, out, chosen = refs[: slabs // 2], refs[-2], refs[-1]
    me = lax.axis_index("slab")
    distance = me ^ jnp.where(me < slabs // 2, 0, slabs - 1)
    zr, zi, _, _ = scalars_of(pole)
    for k, ref in enumerate(near):

        @pl.when(distance == k)
        def _(ref=ref):
            chosen[...] = ref[...]

    (inverse,) = inverses_of(shifted(unpack(chosen[...]), zr, zi))
    put(out, inverse)


def chain(slabs, me, blocks, links, zr, zi):
    left = me < slabs // 2

    def block(own, j):
        index = jnp.where(left == own, j, slabs - 1 - j)
        return shifted(unpack(blocks[index]), zr, zi)

    def reduced(own, j, inverse):
        from_left = left == own
        k = turned_if(jnp.logical_not(from_left), get(links, jnp.where(from_left, j, slabs - j)))
        out, back = times(inverse, k), adjoint(k)
        return times(back, out), out, back

    return block, reduced


def fill_near(me, target, refs):
    for k, ref in enumerate(refs):
        target[me ^ k] = ref[...] if ref.ndim == target.ndim - 1 else ref[0]


def fill_far(me, target, refs):
    middle, core = target.shape[0] // 2, lax.axis_index("sub")
    for i, ref in enumerate(refs):
        mask = middle + i - i % 2 + jnp.where(i % 2 == 0, core, 1 - core)
        target[me ^ mask] = ref[...] if ref.ndim == target.ndim - 1 else ref[0]


def advance(slabs, pole, start, *refs):
    middle = slabs // 2
    block_refs, link_refs, refs = refs[:slabs], refs[slabs : slabs + middle], refs[slabs + middle :]
    here, there, outward, inward, blocks, links = refs
    me = lax.axis_index("slab")
    zr, zi, _, _ = scalars_of(pole)
    fill_near(me, blocks, block_refs[:middle])
    fill_far(me, blocks, block_refs[middle:])
    fill_near(me, links, link_refs)
    block, reduced = chain(slabs, me, blocks, links, zr, zi)
    inverse = get(start)
    taken, out, back = reduced(True, 1, inverse)
    put(outward, out)
    put(inward, times(back, inverse))
    own, other = inverses_of(minus(block(True, 1), taken), block(False, 0))
    put(here, own)
    put(there, other)


def finish(slabs, poles, pole, start, second, end, outward_1, inward_1, *refs):
    middle = slabs // 2
    block_refs, link_refs, refs = refs[:slabs], refs[slabs : 2 * slabs], refs[2 * slabs :]
    outs, (blocks, links, outward, inward, own, other, work) = refs[:poles], refs[poles:]
    me, mine = lax.axis_index("slab"), lax.axis_index(("pole", "sub"))
    order = start.shape[-1]
    fill_near(me, blocks, block_refs[:middle])
    fill_far(me, blocks, block_refs[middle:])
    fill_near(me, links, link_refs[:middle])
    fill_far(me, links, link_refs[middle:])
    zr, zi, wr, wi = scalars_of(pole)
    block, reduced = chain(slabs, me, blocks, links, zr, zi)
    own[0], own[1], other[0] = start[...], second[...], end[...]
    outward[1], inward[1] = outward_1[...], inward_1[...]

    def other_pivot(j):
        return minus(block(False, j), reduced(False, j, get(other, j - 1))[0])

    def level(j, _):
        inverse = get(own, j - 1)
        taken, out, back = reduced(True, j, inverse)
        one, two = inverses_of(minus(block(True, j), taken), other_pivot(j - 1))
        put(outward, out, j)
        put(inward, times(back, inverse), j)
        put(own, one, j)
        put(other, two, j - 1)
        return 0

    def wider(j, found):
        base, out, back = found
        near_out, near_back = get(outward, j), get(inward, j)
        base = plus(get(own, j - 1), times(times(near_out, base), near_back))
        return base, times(near_out, out), times(back, near_back)

    if middle > 2:
        lax.fori_loop(2, middle, level, 0)
    inverse = get(own, middle - 1)
    taken, out, back = reduced(True, middle, inverse)
    steps = middle - 1 - jnp.where(me < middle, me, slabs - 1 - me)
    pivot = minus(other_pivot(middle - 1), taken)
    if middle == 2:
        made = {}

        def aside(name, make):
            return lambda: made.update({name: make()})

        near_out, near_back = get(outward, 1), get(inward, 1)
        asides = [
            aside("back", lambda: times(back, inverse)),
            aside("half", lambda: times(near_out, inverse)),
            aside("further_out", lambda: times(near_out, out)),
            aside("base", lambda: plus(get(own, 0), times(made["half"], near_back))),
            aside("further_back", lambda: times(made["back"], near_back)),
        ]
        (green,) = inverses_of(pivot, asides=asides)
        found = jax.tree.map(
            lambda new, old: jnp.where(steps > 0, new, old),
            (made["base"], made["further_out"], made["further_back"]),
            (inverse, out, made["back"]),
        )
    else:
        found = inverse, out, times(back, inverse)
        found = lax.fori_loop(0, steps, lambda step, found: wider(middle - 1 - step, found), found)
        (green,) = inverses_of(pivot)
    gr, gi = plus(found[0], times(times(found[1], green), found[2]))
    gr_t, gi_t = gr.T, gi.T
    even, odd = (0.5 * (gr + gr_t), 0.5 * (gi + gi_t)), (0.5 * (gr_t - gr), 0.5 * (gi_t - gi))
    rows = order // poles
    for slot, (ur, ui) in enumerate(((wr, wi), (wr * zr - wi * zi, wr * zi + wi * zr))):
        put(work, (ur * even[1] + ui * even[0], ur * odd[0] - ui * odd[1]), slot)
    for k in range(poles):
        begin = pl.multiple_of((mine ^ k) * rows, rows)
        outs[k][...] = work[:, :, pl.ds(begin, rows), :]


def shards(slabs, poles, onsite, coupling, pole_real, pole_imag, pole_weight):
    order = onsite.shape[-1]
    middle = slabs // 2
    vmem = pl.BlockSpec(memory_space=pltpu.VMEM)
    params = pltpu.CompilerParams(vmem_limit_bytes=40 << 20)
    square_of = jax.ShapeDtypeStruct((order, order), f32)
    complex_of = jax.ShapeDtypeStruct((2, order, order), f32)

    def scratch(*lead):
        return pltpu.VMEM((*lead, order, order), f32)

    def cost(inversions):
        return pl.CostEstimate(
            flops=inversions * 25 * 10**8, bytes_accessed=inversions * 10**6, transcendentals=0
        )

    def swap(value, k):
        return lax.ppermute(value, "slab", [(i, i ^ k) for i in range(slabs)])

    packed = pl.pallas_call(
        prepare, out_shape=square_of, in_specs=[vmem], out_specs=vmem, compiler_params=params
    )(onsite)
    pole = pl.pallas_call(
        spread_scalars,
        out_shape=jax.ShapeDtypeStruct((ROWS, order), f32),
        in_specs=[vmem] * 3,
        out_specs=vmem,
        compiler_params=params,
    )(pole_real, pole_imag, pole_weight)

    def far_swap(value, k):
        pairs = [(2 * i + c, 2 * (i ^ (k + c)) + c) for i in range(slabs) for c in range(2)]
        return lax.ppermute(value, ("slab", "sub"), pairs)

    near_blocks = [packed] + [swap(packed, k) for k in range(1, middle)]
    far_blocks = [far_swap(packed, k) for k in range(middle, slabs, 2)]
    near_links = [coupling] + [swap(coupling, k) for k in range(1, middle)]
    far_links = [far_swap(coupling, k) for k in range(middle, slabs, 2)]
    start = pl.pallas_call(
        functools.partial(start_chain, slabs),
        out_shape=complex_of,
        in_specs=[vmem] * (1 + middle),
        out_specs=vmem,
        scratch_shapes=[scratch()],
        compiler_params=params,
        cost_estimate=cost(2),
    )(pole, *near_blocks)

    def both(values, after):
        pairs = []
        for value in values:
            mine, _ = lax.optimization_barrier((value, after))
            pairs += [value, lax.ppermute(mine, "sub", [(0, 1), (1, 0)])]
        return pairs

    blocks = near_blocks + both(far_blocks, start)
    second = pl.pallas_call(
        functools.partial(advance, slabs),
        out_shape=[complex_of] * 4,
        in_specs=[vmem] * (2 + slabs + middle),
        out_specs=[vmem] * 4,
        scratch_shapes=[scratch(slabs), scratch(slabs, 2)],
        compiler_params=params,
        cost_estimate=pl.CostEstimate(flops=1000, bytes_accessed=1000, transcendentals=0),
    )(pole, start, *blocks, *near_links)
    links = near_links + both(far_links, second[0])
    pieces = pl.pallas_call(
        functools.partial(finish, slabs, poles),
        out_shape=[jax.ShapeDtypeStruct((2, 2, order // poles, order), f32)] * poles,
        in_specs=[vmem] * (6 + 2 * slabs),
        out_specs=[vmem] * poles,
        scratch_shapes=[
            scratch(slabs),
            scratch(slabs, 2),
            scratch(middle + 1, 2),
            scratch(middle + 1, 2),
            scratch(middle, 2),
            scratch(middle, 2),
            scratch(2, 2),
        ],
        compiler_params=params,
        cost_estimate=cost(2),
    )(pole, start, *second, *blocks, *links)
    total = pieces[0]
    for k in range(1, poles):
        total = total + lax.ppermute(pieces[k], ("pole", "sub"), [(i, i ^ k) for i in range(poles)])
    return total[0][None], total[1][None]


def solution(mesh):
    in_specs = (
        P(("groups", "slab"), None, None, None),
        P(("groups", "slab"), None, None, None),
        P(("pole", "sub")),
        P(("pole", "sub")),
        P(("pole", "sub"), None),
    )
    out_specs = (
        P(("groups", "slab"), None, ("pole", "sub"), None),
        P(("groups", "slab"), None, ("pole", "sub"), None),
    )
    body = functools.partial(shards, mesh.shape["slab"], mesh.shape["pole"] * mesh.shape["sub"])
    return jax.shard_map(body, mesh=mesh, in_specs=in_specs, out_specs=out_specs, check_vma=False)
```

```python
import functools

import jax
import jax.numpy as jnp
from jax import lax
from jax.experimental import pallas as pl
from jax.experimental.pallas import tpu as pltpu
from jax.sharding import PartitionSpec as P

ROWS = 8
PANEL = 2 * ROWS
f32, bf16 = jnp.float32, jnp.bfloat16
PARTS = ((0, 0), (1, 0), (0, 1), (1, 1), (0, 2), (2, 0))


def row_of(tile, k):
    return jnp.broadcast_to(tile[k : k + 1, :], tile.shape)


def lane_of(tile, k):
    where = jnp.full(tile.shape, k, jnp.int32)
    return jnp.take_along_axis(tile, where, axis=1, mode="promise_in_bounds")


def plus(a, b):
    return a[0] + b[0], a[1] + b[1]


def minus(a, b):
    return a[0] - b[0], a[1] - b[1]


def complex_times(a, b):
    return a[0] * b[0] - a[1] * b[1], a[0] * b[1] + a[1] * b[0]


def sweep_double(tiles, columns, first, lane, subl):
    tiles = list(tiles)
    columns = [list(cols) for cols in columns]
    for k in range(0, ROWS, 2):
        for s, cols in enumerate(columns):

            def entries(pair):
                return [(row_of(pair[0], i), row_of(pair[1], i)) for i in (k, k + 1)]

            (a, c), (b, d) = entries(cols[k]), entries(cols[k + 1])
            det = minus(complex_times(a, d), complex_times(b, c))
            scale = 1.0 / (det[0] * det[0] + det[1] * det[1])
            over = det[0] * scale, -det[1] * scale
            one = cols[k][0] - (subl == k).astype(f32), cols[k][1]
            two = cols[k + 1][0] - (subl == k + 1).astype(f32), cols[k + 1][1]
            one, two = (
                minus(complex_times(one, d), complex_times(two, c)),
                minus(complex_times(two, a), complex_times(one, b)),
            )
            for j in range(k + 2, min(k + 3, ROWS)):
                upper, lower = entries(cols[j])
                taken = plus(complex_times(one, upper), complex_times(two, lower))
                cols[j] = minus(cols[j], complex_times(taken, over))
            one, two = complex_times(one, over), complex_times(two, over)
            for j in range(k + 3, ROWS):
                upper, lower = entries(cols[j])
                cols[j] = minus(cols[j], plus(complex_times(one, upper), complex_times(two, lower)))
            upper, lower = entries(tiles[s])
            upper = upper[0] + (lane == first + k).astype(f32), upper[1]
            lower = lower[0] + (lane == first + k + 1).astype(f32), lower[1]
            tiles[s] = minus(tiles[s], plus(complex_times(one, upper), complex_times(two, lower)))
    return tiles


def sweep_single(tiles, columns, first, lane, subl):
    tiles = list(tiles)
    columns = [list(cols) for cols in columns]
    for k in range(ROWS):
        in_row, in_lane = (subl == k).astype(f32), (lane == first + k).astype(f32)
        for s, cols in enumerate(columns):
            xr, xi = tiles[s]
            tr, ti = cols[k]
            dr, di = row_of(tr, k), row_of(ti, k)
            scale = 1.0 / (dr * dr + di * di)
            rr, ri = dr * scale, -di * scale
            cr = tr - in_row
            cr, ci = cr * rr - ti * ri, cr * ri + ti * rr
            for j in range(k + 1, ROWS):
                ar, ai = row_of(cols[j][0], k), row_of(cols[j][1], k)
                cols[j] = (cols[j][0] - (cr * ar - ci * ai), cols[j][1] - (cr * ai + ci * ar))
            ar, ai = row_of(xr, k) + in_lane, row_of(xi, k)
            tiles[s] = (xr - (cr * ar - ci * ai), xi - (cr * ai + ci * ar))
    return tiles


def spread(tiles, first):
    return [
        [(lane_of(xr, first + k), lane_of(xi, first + k)) for k in range(ROWS)] for xr, xi in tiles
    ]


def follow(tile, columns, swept, inside):
    nr, ni = jnp.where(inside, 0.0, tile[0]), jnp.where(inside, 0.0, tile[1])
    pr = pi = None
    for k, column in enumerate(columns):
        tr, ti = complex_times(column, (row_of(swept[0], k), row_of(swept[1], k)))
        if k % 2 == 0:
            nr, ni = nr - tr, ni - ti
        else:
            pr, pi = (tr, ti) if pr is None else (pr + tr, pi + ti)
    return nr - pr, ni - pi


def follow_all(tiles, columns, swept, inside, after=None):
    if after is None or len(tiles) > 1:
        masks = [inside] * len(tiles)
    else:
        masks = [inside & (tile[1] == tile[1]) for tile in after]
    return [follow(*args) for args in zip(tiles, columns, swept, masks)]


def split(x):
    parts = [x.astype(bf16)]
    for _ in range(2):
        x = x - parts[-1].astype(f32)
        parts.append(x.astype(bf16))
    return parts


def multiply(left, right, columns):
    rows = left[0][0].shape[0]
    lhs = jnp.concatenate(
        [jnp.concatenate((left[0][a], left[1][a]), axis=0) for a, _ in PARTS], axis=1
    )
    rhs = jnp.concatenate(
        [jnp.concatenate((right[0][b], right[1][b]), axis=1) for _, b in PARTS], axis=0
    )
    whole = lax.dot_general(lhs, rhs, (((1,), (0,)), ((), ())), preferred_element_type=f32)
    return (
        whole[:rows, :columns] - whole[rows:, columns:],
        whole[:rows, columns:] + whole[rows:, :columns],
    )


def times(left, right):
    columns = right[0].shape[1]
    return multiply([split(part) for part in left], [split(part) for part in right], columns)


def others_follow(tiles, panel, place):
    order = tiles[0][0].shape[1]

    def padded(rows):
        above, below = PANEL * place, order - PANEL * (place + 1)
        parts = [jnp.zeros((above, order), bf16)] if above else []
        parts += [rows]
        parts += [jnp.zeros((below, order), bf16)] if below else []
        return jnp.concatenate(parts, axis=0)

    left = [split(jnp.concatenate(part, axis=0)) for part in zip(*tiles)]
    right = [[padded(rows) for rows in split(jnp.concatenate(part, axis=0))] for part in zip(*panel)]
    real, imag = multiply(left, right, order)
    return [(real[ROWS * t : ROWS * t + ROWS], imag[ROWS * t : ROWS * t + ROWS]) for t in range(len(tiles))]


def invert(systems, asides):
    order = systems[0][0][0].shape[1]
    count, panels = order // ROWS, order // PANEL
    lane = lax.broadcasted_iota(jnp.int32, (ROWS, order), 1)
    subl = lax.broadcasted_iota(jnp.int32, (ROWS, order), 0)
    systems = [list(tiles) for tiles in systems]
    sweep = sweep_double if len(systems) == 1 else sweep_single
    for place in range(panels):
        a, b = 2 * place, 2 * place + 1
        in_a = (lane >= ROWS * a) & (lane < ROWS * a + ROWS)
        in_b = (lane >= ROWS * b) & (lane < ROWS * b + ROWS)
        soon = [] if place == panels - 1 else [b + 1, b + 2]
        nexts = [[tiles[i] for tiles in systems] for i in soon]
        second = [tiles[b] for tiles in systems]
        if place == 0:
            columns = spread([tiles[a] for tiles in systems], ROWS * a)
        second_columns = spread(second, ROWS * a)
        next_columns = [spread(tiles, ROWS * a) for tiles in nexts]
        first = sweep([tiles[a] for tiles in systems], columns, ROWS * a, lane, subl)
        second = follow_all(second, second_columns, first, in_a)
        columns = spread(second, ROWS * b)
        nexts = [follow_all(tiles, cols, first, in_a, second) for tiles, cols in zip(nexts, next_columns)]
        next_columns = [spread(tiles, ROWS * b) for tiles in nexts]
        first_columns = spread(first, ROWS * b)
        second = sweep(second, columns, ROWS * b, lane, subl)
        for i, cols in enumerate(next_columns):
            nexts[i] = follow_all(nexts[i], cols, second, in_b, nexts[0] if i else None)
            if i == 0:
                columns = spread(nexts[0], ROWS * (b + 1))
        first = follow_all(first, first_columns, second, in_b, nexts[0] if nexts else None)
        rest = [i for i in range(count) if i not in (a, b, *soon)]
        rest.sort(key=lambda i: (i - b) % count)
        for s, tiles in enumerate(systems):
            delta = others_follow([tiles[i] for i in rest], [first[s], second[s]], place)
            for (dr, di), i in zip(delta, rest):
                tiles[i] = (
                    jnp.where(in_a | in_b, 0.0, tiles[i][0]) - dr,
                    jnp.where(in_a | in_b, 0.0, tiles[i][1]) - di,
                )
            tiles[a], tiles[b] = first[s], second[s]
            for i, tile in zip(soon, nexts):
                tiles[i] = tile[s]
        if place < len(asides):
            asides[place]()
    return systems


def to_tiles(value):
    count = value[0].shape[0] // ROWS
    return [tuple(part[ROWS * i : ROWS * i + ROWS] for part in value) for i in range(count)]


def from_tiles(tiles):
    return tuple(jnp.concatenate(part, axis=0) for part in zip(*tiles))


def inverses_of(*values, asides=()):
    return [from_tiles(tiles) for tiles in invert([to_tiles(value) for value in values], asides)]


def adjoint(a):
    return a[0].T, -a[1].T


def get(ref, *index):
    return ref[(*index, 0)], ref[(*index, 1)]


def put(ref, value, *index):
    ref[(*index, 0)], ref[(*index, 1)] = value


def square(order):
    rows = lax.broadcasted_iota(jnp.int32, (order, order), 0)
    columns = lax.broadcasted_iota(jnp.int32, (order, order), 1)
    return rows, columns


def hermitian(onsite):
    return 0.5 * (onsite[0] + onsite[0].T), 0.5 * (onsite[1] - onsite[1].T)


def pack(block):
    rows, columns = square(block[0].shape[0])
    return jnp.where(rows <= columns, *block)


def unpack(packed):
    rows, columns = square(packed.shape[0])
    turned = packed.T
    imag = jnp.where(rows > columns, packed, jnp.where(rows < columns, -turned, 0.0))
    return jnp.where(rows <= columns, packed, turned), imag


def shifted(block, zr, zi):
    rows, columns = square(block[0].shape[0])
    return jnp.where(rows == columns, block[0] - zr, block[0]), jnp.where(rows == columns, -zi, block[1])


def prepare(onsite, packed):
    packed[...] = pack(hermitian(get(onsite, 0)))


def spread_scalars(pole_real, pole_imag, pole_weight, pole):
    width = pole.shape[1]
    pole[0:1, :] = jnp.broadcast_to(pole_real[...].reshape(1, 1), (1, width))
    pole[1:2, :] = jnp.broadcast_to(pole_imag[...].reshape(1, 1), (1, width))
    pole[2:3, :] = jnp.broadcast_to(pole_weight[:, 0:1], (1, width))
    pole[3:4, :] = jnp.broadcast_to(pole_weight[:, 1:2], (1, width))


def halve(coupling, half):
    half[...] = coupling[0, lax.axis_index("sub")]


def scalars_of(pole):
    return [pole[row : row + 1, :] for row in range(4)]


def turned_if(turn, value):
    return jnp.where(turn, value[0].T, value[0]), jnp.where(turn, -value[1].T, value[1])


def start_chain(slabs, pole, *refs):
    near, out, chosen = refs[: slabs // 2], refs[-2], refs[-1]
    me = lax.axis_index("slab")
    distance = me ^ jnp.where(me < slabs // 2, 0, slabs - 1)
    zr, zi, _, _ = scalars_of(pole)
    for k, ref in enumerate(near):

        @pl.when(distance == k)
        def _(ref=ref):
            chosen[...] = ref[...]

    (inverse,) = inverses_of(shifted(unpack(chosen[...]), zr, zi))
    put(out, inverse)


def chain(slabs, me, blocks, links, zr, zi):
    left = me < slabs // 2

    def block(own, j):
        index = jnp.where(left == own, j, slabs - 1 - j)
        return shifted(unpack(blocks[index]), zr, zi)

    def reduced(own, j, inverse):
        from_left = left == own
        k = turned_if(jnp.logical_not(from_left), get(links, jnp.where(from_left, j, slabs - j)))
        out, back = times(inverse, k), adjoint(k)
        return times(back, out), out, back

    return block, reduced


def fill_near(me, target, refs):
    for k, ref in enumerate(refs):
        target[me ^ k] = ref[...] if ref.ndim == target.ndim - 1 else ref[0]


def fill_links(me, target, own, halves):
    core = lax.axis_index("sub")
    target[me] = own[0]
    for i, ref in enumerate(halves):
        target[me ^ (1 + i // 2), core if i % 2 == 0 else 1 - core] = ref[...]


def fill_far(me, target, refs):
    middle, core = target.shape[0] // 2, lax.axis_index("sub")
    for i, ref in enumerate(refs):
        mask = middle + i - i % 2 + jnp.where(i % 2 == 0, core, 1 - core)
        target[me ^ mask] = ref[...] if ref.ndim == target.ndim - 1 else ref[0]


def couple(slabs, pole, start, *refs):
    middle = slabs // 2
    block_refs, own, refs = refs[:middle], refs[middle], refs[middle + 1 :]
    halves, refs = refs[: 2 * middle - 2], refs[2 * middle - 2 :]
    pivot, outward, inward, blocks, links = refs
    me = lax.axis_index("slab")
    zr, zi, _, _ = scalars_of(pole)
    fill_near(me, blocks, block_refs)
    fill_links(me, links, own, halves)
    block, reduced = chain(slabs, me, blocks, links, zr, zi)
    inverse = get(start)
    taken, out, back = reduced(True, 1, inverse)
    put(pivot, minus(block(True, 1), taken))
    put(outward, out)
    put(inward, times(back, inverse))


def advance(slabs, pole, pivot, *refs):
    middle = slabs // 2
    block_refs, (here, there, blocks) = refs[:middle], refs[middle:]
    me = lax.axis_index("slab")
    zr, zi, _, _ = scalars_of(pole)
    fill_far(me, blocks, block_refs)
    block, _ = chain(slabs, me, blocks, None, zr, zi)
    own, other = inverses_of(get(pivot), block(False, 0))
    put(here, own)
    put(there, other)


def finish(slabs, poles, pole, start, second, end, outward_1, inward_1, *refs):
    middle = slabs // 2
    block_refs, coupling, refs = refs[:slabs], refs[slabs], refs[slabs + 1 :]
    halves, refs = refs[: 2 * middle - 2], refs[2 * middle - 2 :]
    far_refs, refs = refs[:middle], refs[middle:]
    outs, (blocks, links, outward, inward, own, other, work) = refs[:poles], refs[poles:]
    me, mine = lax.axis_index("slab"), lax.axis_index(("pole", "sub"))
    order = start.shape[-1]
    fill_near(me, blocks, block_refs[:middle])
    fill_far(me, blocks, block_refs[middle:])
    fill_links(me, links, coupling, halves)
    fill_far(me, links, far_refs)
    zr, zi, wr, wi = scalars_of(pole)
    block, reduced = chain(slabs, me, blocks, links, zr, zi)
    own[0], own[1], other[0] = start[...], second[...], end[...]
    outward[1], inward[1] = outward_1[...], inward_1[...]

    def other_pivot(j):
        return minus(block(False, j), reduced(False, j, get(other, j - 1))[0])

    def level(j, _):
        inverse = get(own, j - 1)
        taken, out, back = reduced(True, j, inverse)
        one, two = inverses_of(minus(block(True, j), taken), other_pivot(j - 1))
        put(outward, out, j)
        put(inward, times(back, inverse), j)
        put(own, one, j)
        put(other, two, j - 1)
        return 0

    def wider(j, found):
        base, out, back = found
        near_out, near_back = get(outward, j), get(inward, j)
        base = plus(get(own, j - 1), times(times(near_out, base), near_back))
        return base, times(near_out, out), times(back, near_back)

    if middle > 2:
        lax.fori_loop(2, middle, level, 0)
    inverse = get(own, middle - 1)
    taken, out, back = reduced(True, middle, inverse)
    steps = middle - 1 - jnp.where(me < middle, me, slabs - 1 - me)
    pivot = minus(other_pivot(middle - 1), taken)
    if middle == 2:
        made = {}

        def aside(name, make):
            return lambda: made.update({name: make()})

        near_out, near_back = get(outward, 1), get(inward, 1)
        asides = [
            aside("back", lambda: times(back, inverse)),
            aside("half", lambda: times(near_out, inverse)),
            aside("further_out", lambda: times(near_out, out)),
            aside("base", lambda: plus(get(own, 0), times(made["half"], near_back))),
            aside("further_back", lambda: times(made["back"], near_back)),
        ]
        (green,) = inverses_of(pivot, asides=asides)
        found = jax.tree.map(
            lambda new, old: jnp.where(steps > 0, new, old),
            (made["base"], made["further_out"], made["further_back"]),
            (inverse, out, made["back"]),
        )
    else:
        found = inverse, out, times(back, inverse)
        found = lax.fori_loop(0, steps, lambda step, found: wider(middle - 1 - step, found), found)
        (green,) = inverses_of(pivot)
    gr, gi = plus(found[0], times(times(found[1], green), found[2]))
    gr_t, gi_t = gr.T, gi.T
    even, odd = (0.5 * (gr + gr_t), 0.5 * (gi + gi_t)), (0.5 * (gr_t - gr), 0.5 * (gi_t - gi))
    rows = order // poles
    for slot, (ur, ui) in enumerate(((wr, wi), (wr * zr - wi * zi, wr * zi + wi * zr))):
        put(work, (ur * even[1] + ui * even[0], ur * odd[0] - ui * odd[1]), slot)
    for k in range(poles):
        begin = pl.multiple_of((mine ^ k) * rows, rows)
        outs[k][...] = work[:, :, pl.ds(begin, rows), :]


def shards(slabs, poles, onsite, coupling, pole_real, pole_imag, pole_weight):
    order = onsite.shape[-1]
    middle = slabs // 2
    vmem = pl.BlockSpec(memory_space=pltpu.VMEM)
    params = pltpu.CompilerParams(vmem_limit_bytes=40 << 20)
    square_of = jax.ShapeDtypeStruct((order, order), f32)
    complex_of = jax.ShapeDtypeStruct((2, order, order), f32)

    def scratch(*lead):
        return pltpu.VMEM((*lead, order, order), f32)

    def cost(inversions):
        return pl.CostEstimate(
            flops=inversions * 25 * 10**8, bytes_accessed=inversions * 10**6, transcendentals=0
        )

    def swap(value, k):
        return lax.ppermute(value, "slab", [(i, i ^ k) for i in range(slabs)])

    half = pl.pallas_call(
        halve, out_shape=square_of, in_specs=[vmem], out_specs=vmem, compiler_params=params
    )(coupling)
    near_links = [swap(half, k) for k in range(1, middle)]
    packed = pl.pallas_call(
        prepare, out_shape=square_of, in_specs=[vmem], out_specs=vmem, compiler_params=params
    )(onsite)
    pole = pl.pallas_call(
        spread_scalars,
        out_shape=jax.ShapeDtypeStruct((ROWS, order), f32),
        in_specs=[vmem] * 3,
        out_specs=vmem,
        compiler_params=params,
    )(pole_real, pole_imag, pole_weight)

    def far_swap(value, k):
        pairs = [(2 * i + c, 2 * (i ^ (k + c)) + c) for i in range(slabs) for c in range(2)]
        return lax.ppermute(value, ("slab", "sub"), pairs)

    near_blocks = [packed] + [swap(packed, k) for k in range(1, middle)]
    far_blocks = [far_swap(packed, k) for k in range(middle, slabs, 2)]
    far_links = [far_swap(coupling, k) for k in range(middle, slabs, 2)]
    start = pl.pallas_call(
        functools.partial(start_chain, slabs),
        out_shape=complex_of,
        in_specs=[vmem] * (1 + middle),
        out_specs=vmem,
        scratch_shapes=[scratch()],
        compiler_params=params,
        cost_estimate=cost(2),
    )(pole, *near_blocks)

    def both(values, after):
        pairs = []
        for value in values:
            mine, _ = lax.optimization_barrier((value, after))
            pairs += [value, lax.ppermute(mine, "sub", [(0, 1), (1, 0)])]
        return pairs

    far_blocks = both(far_blocks, start)
    near_links = both(near_links, start)
    pivot, *factors = pl.pallas_call(
        functools.partial(couple, slabs),
        out_shape=[complex_of] * 3,
        in_specs=[vmem] * (1 + 3 * middle),
        out_specs=[vmem] * 3,
        scratch_shapes=[scratch(slabs), scratch(slabs, 2)],
        compiler_params=params,
        cost_estimate=pl.CostEstimate(flops=1000, bytes_accessed=1000, transcendentals=0),
    )(pole, start, *near_blocks, coupling, *near_links)
    far_links = both(far_links, pivot)
    second = pl.pallas_call(
        functools.partial(advance, slabs),
        out_shape=[complex_of] * 2,
        in_specs=[vmem] * (2 + middle),
        out_specs=[vmem] * 2,
        scratch_shapes=[scratch(slabs)],
        compiler_params=params,
        cost_estimate=cost(2),
    )(pole, pivot, *far_blocks)
    blocks, links = near_blocks + far_blocks, [coupling] + near_links + far_links
    pieces = pl.pallas_call(
        functools.partial(finish, slabs, poles),
        out_shape=[jax.ShapeDtypeStruct((2, 2, order // poles, order), f32)] * poles,
        in_specs=[vmem] * (5 + 2 * slabs + middle),
        out_specs=[vmem] * poles,
        scratch_shapes=[
            scratch(slabs),
            scratch(slabs, 2),
            scratch(middle + 1, 2),
            scratch(middle + 1, 2),
            scratch(middle, 2),
            scratch(middle, 2),
            scratch(2, 2),
        ],
        compiler_params=params,
        cost_estimate=cost(2),
    )(pole, start, *second, *factors, *blocks, *links)
    total = pieces[0]
    for k in range(1, poles):
        total = total + lax.ppermute(pieces[k], ("pole", "sub"), [(i, i ^ k) for i in range(poles)])
    return total[0][None], total[1][None]


def solution(mesh):
    in_specs = (
        P(("groups", "slab"), None, None, None),
        P(("groups", "slab"), None, None, None),
        P(("pole", "sub")),
        P(("pole", "sub")),
        P(("pole", "sub"), None),
    )
    out_specs = (
        P(("groups", "slab"), None, ("pole", "sub"), None),
        P(("groups", "slab"), None, ("pole", "sub"), None),
    )
    body = functools.partial(shards, mesh.shape["slab"], mesh.shape["pole"] * mesh.shape["sub"])
    return jax.shard_map(body, mesh=mesh, in_specs=in_specs, out_specs=out_specs, check_vma=False)
```

```python
import functools

import jax
import jax.numpy as jnp
from jax import lax
from jax.experimental import pallas as pl
from jax.experimental.pallas import tpu as pltpu
from jax.sharding import PartitionSpec as P

ROWS = 8
PANEL = 2 * ROWS
SPLIT = 2
f32, bf16 = jnp.float32, jnp.bfloat16
PARTS = ((0, 0), (1, 0), (0, 1), (1, 1), (0, 2), (2, 0))


def row_of(tile, k):
    return jnp.broadcast_to(tile[k : k + 1, :], tile.shape)


def lane_of(tile, k):
    where = jnp.full(tile.shape, k, jnp.int32)
    return jnp.take_along_axis(tile, where, axis=1, mode="promise_in_bounds")


def plus(a, b):
    return a[0] + b[0], a[1] + b[1]


def minus(a, b):
    return a[0] - b[0], a[1] - b[1]


def complex_times(a, b):
    return a[0] * b[0] - a[1] * b[1], a[0] * b[1] + a[1] * b[0]


def sweep_double(tiles, columns, first, lane, subl):
    tiles = list(tiles)
    columns = [list(cols) for cols in columns]
    for k in range(0, ROWS, 2):
        for s, cols in enumerate(columns):

            def entries(pair):
                return [(row_of(pair[0], i), row_of(pair[1], i)) for i in (k, k + 1)]

            (a, c), (b, d) = entries(cols[k]), entries(cols[k + 1])
            det = minus(complex_times(a, d), complex_times(b, c))
            scale = 1.0 / (det[0] * det[0] + det[1] * det[1])
            over = det[0] * scale, -det[1] * scale
            one = cols[k][0] - (subl == k).astype(f32), cols[k][1]
            two = cols[k + 1][0] - (subl == k + 1).astype(f32), cols[k + 1][1]
            one, two = (
                minus(complex_times(one, d), complex_times(two, c)),
                minus(complex_times(two, a), complex_times(one, b)),
            )
            for j in range(k + 2, min(k + 3, ROWS)):
                upper, lower = entries(cols[j])
                taken = plus(complex_times(one, upper), complex_times(two, lower))
                cols[j] = minus(cols[j], complex_times(taken, over))
            one, two = complex_times(one, over), complex_times(two, over)
            for j in range(k + 3, ROWS):
                upper, lower = entries(cols[j])
                cols[j] = minus(cols[j], plus(complex_times(one, upper), complex_times(two, lower)))
            upper, lower = entries(tiles[s])
            upper = upper[0] + (lane == first + k).astype(f32), upper[1]
            lower = lower[0] + (lane == first + k + 1).astype(f32), lower[1]
            tiles[s] = minus(tiles[s], plus(complex_times(one, upper), complex_times(two, lower)))
    return tiles


def sweep_single(tiles, columns, first, lane, subl):
    tiles = list(tiles)
    columns = [list(cols) for cols in columns]
    for k in range(ROWS):
        in_row, in_lane = (subl == k).astype(f32), (lane == first + k).astype(f32)
        for s, cols in enumerate(columns):
            xr, xi = tiles[s]
            tr, ti = cols[k]
            dr, di = row_of(tr, k), row_of(ti, k)
            scale = 1.0 / (dr * dr + di * di)
            rr, ri = dr * scale, -di * scale
            cr = tr - in_row
            cr, ci = cr * rr - ti * ri, cr * ri + ti * rr
            for j in range(k + 1, ROWS):
                ar, ai = row_of(cols[j][0], k), row_of(cols[j][1], k)
                cols[j] = (cols[j][0] - (cr * ar - ci * ai), cols[j][1] - (cr * ai + ci * ar))
            ar, ai = row_of(xr, k) + in_lane, row_of(xi, k)
            tiles[s] = (xr - (cr * ar - ci * ai), xi - (cr * ai + ci * ar))
    return tiles


def spread(tiles, first):
    return [
        [(lane_of(xr, first + k), lane_of(xi, first + k)) for k in range(ROWS)] for xr, xi in tiles
    ]


def follow(tile, columns, swept, inside):
    nr, ni = jnp.where(inside, 0.0, tile[0]), jnp.where(inside, 0.0, tile[1])
    pr = pi = None
    for k, column in enumerate(columns):
        tr, ti = complex_times(column, (row_of(swept[0], k), row_of(swept[1], k)))
        if k % 2 == 0:
            nr, ni = nr - tr, ni - ti
        else:
            pr, pi = (tr, ti) if pr is None else (pr + tr, pi + ti)
    return nr - pr, ni - pi


def follow_all(tiles, columns, swept, inside, after=None):
    if after is None or len(tiles) > 1:
        masks = [inside] * len(tiles)
    else:
        masks = [inside & (tile[1] == tile[1]) for tile in after]
    return [follow(*args) for args in zip(tiles, columns, swept, masks)]


def split(x):
    parts = [x.astype(bf16)]
    for _ in range(2):
        x = x - parts[-1].astype(f32)
        parts.append(x.astype(bf16))
    return parts


def multiply(left, right, columns):
    rows = left[0][0].shape[0]
    lhs = jnp.concatenate(
        [jnp.concatenate((left[0][a], left[1][a]), axis=0) for a, _ in PARTS], axis=1
    )
    rhs = jnp.concatenate(
        [jnp.concatenate((right[0][b], right[1][b]), axis=1) for _, b in PARTS], axis=0
    )
    whole = lax.dot_general(lhs, rhs, (((1,), (0,)), ((), ())), preferred_element_type=f32)
    return (
        whole[:rows, :columns] - whole[rows:, columns:],
        whole[:rows, columns:] + whole[rows:, :columns],
    )


def times(left, right):
    columns = right[0].shape[1]
    return multiply([split(part) for part in left], [split(part) for part in right], columns)


def others_follow(tiles, panel, place):
    order = tiles[0][0].shape[1]

    def padded(rows):
        above, below = PANEL * place, order - PANEL * (place + 1)
        parts = [jnp.zeros((above, order), bf16)] if above else []
        parts += [rows]
        parts += [jnp.zeros((below, order), bf16)] if below else []
        return jnp.concatenate(parts, axis=0)

    left = [split(jnp.concatenate(part, axis=0)) for part in zip(*tiles)]
    right = [[padded(rows) for rows in split(jnp.concatenate(part, axis=0))] for part in zip(*panel)]
    real, imag = multiply(left, right, order)
    return [(real[ROWS * t : ROWS * t + ROWS], imag[ROWS * t : ROWS * t + ROWS]) for t in range(len(tiles))]


def invert(systems, asides=(), begin=0, end=None):
    order = systems[0][0][0].shape[1]
    count, panels = order // ROWS, order // PANEL
    lane = lax.broadcasted_iota(jnp.int32, (ROWS, order), 1)
    subl = lax.broadcasted_iota(jnp.int32, (ROWS, order), 0)
    systems = [list(tiles) for tiles in systems]
    sweep = sweep_double if len(systems) == 1 else sweep_single
    for place in range(panels)[begin:end]:
        a, b = 2 * place, 2 * place + 1
        in_a = (lane >= ROWS * a) & (lane < ROWS * a + ROWS)
        in_b = (lane >= ROWS * b) & (lane < ROWS * b + ROWS)
        soon = [] if place == panels - 1 else [b + 1, b + 2]
        nexts = [[tiles[i] for tiles in systems] for i in soon]
        second = [tiles[b] for tiles in systems]
        if place == begin:
            columns = spread([tiles[a] for tiles in systems], ROWS * a)
        second_columns = spread(second, ROWS * a)
        next_columns = [spread(tiles, ROWS * a) for tiles in nexts]
        first = sweep([tiles[a] for tiles in systems], columns, ROWS * a, lane, subl)
        second = follow_all(second, second_columns, first, in_a)
        columns = spread(second, ROWS * b)
        nexts = [follow_all(tiles, cols, first, in_a, second) for tiles, cols in zip(nexts, next_columns)]
        next_columns = [spread(tiles, ROWS * b) for tiles in nexts]
        first_columns = spread(first, ROWS * b)
        second = sweep(second, columns, ROWS * b, lane, subl)
        for i, cols in enumerate(next_columns):
            nexts[i] = follow_all(nexts[i], cols, second, in_b, nexts[0] if i else None)
            if i == 0:
                columns = spread(nexts[0], ROWS * (b + 1))
        first = follow_all(first, first_columns, second, in_b, nexts[0] if nexts else None)
        rest = [i for i in range(count) if i not in (a, b, *soon)]
        rest.sort(key=lambda i: (i - b) % count)
        for s, tiles in enumerate(systems):
            delta = others_follow([tiles[i] for i in rest], [first[s], second[s]], place)
            for (dr, di), i in zip(delta, rest):
                tiles[i] = (
                    jnp.where(in_a | in_b, 0.0, tiles[i][0]) - dr,
                    jnp.where(in_a | in_b, 0.0, tiles[i][1]) - di,
                )
            tiles[a], tiles[b] = first[s], second[s]
            for i, tile in zip(soon, nexts):
                tiles[i] = tile[s]
        if place < len(asides):
            asides[place]()
    return systems


def to_tiles(value):
    count = value[0].shape[0] // ROWS
    return [tuple(part[ROWS * i : ROWS * i + ROWS] for part in value) for i in range(count)]


def from_tiles(tiles):
    return tuple(jnp.concatenate(part, axis=0) for part in zip(*tiles))


def inverses_of(*values, asides=()):
    return [from_tiles(tiles) for tiles in invert([to_tiles(value) for value in values], asides)]


def adjoint(a):
    return a[0].T, -a[1].T


def get(ref, *index):
    return ref[(*index, 0)], ref[(*index, 1)]


def put(ref, value, *index):
    ref[(*index, 0)], ref[(*index, 1)] = value


def square(order):
    rows = lax.broadcasted_iota(jnp.int32, (order, order), 0)
    columns = lax.broadcasted_iota(jnp.int32, (order, order), 1)
    return rows, columns


def hermitian(onsite):
    return 0.5 * (onsite[0] + onsite[0].T), 0.5 * (onsite[1] - onsite[1].T)


def pack(block):
    rows, columns = square(block[0].shape[0])
    return jnp.where(rows <= columns, *block)


def unpack(packed):
    rows, columns = square(packed.shape[0])
    turned = packed.T
    imag = jnp.where(rows > columns, packed, jnp.where(rows < columns, -turned, 0.0))
    return jnp.where(rows <= columns, packed, turned), imag


def shifted(block, zr, zi):
    rows, columns = square(block[0].shape[0])
    return jnp.where(rows == columns, block[0] - zr, block[0]), jnp.where(rows == columns, -zi, block[1])


def prepare(onsite, packed):
    packed[...] = pack(hermitian(get(onsite, 0)))


def spread_scalars(pole_real, pole_imag, pole_weight, pole):
    width = pole.shape[1]
    pole[0:1, :] = jnp.broadcast_to(pole_real[...].reshape(1, 1), (1, width))
    pole[1:2, :] = jnp.broadcast_to(pole_imag[...].reshape(1, 1), (1, width))
    pole[2:3, :] = jnp.broadcast_to(pole_weight[:, 0:1], (1, width))
    pole[3:4, :] = jnp.broadcast_to(pole_weight[:, 1:2], (1, width))


def halve(coupling, half):
    half[...] = coupling[0, lax.axis_index("sub")]


def scalars_of(pole):
    return [pole[row : row + 1, :] for row in range(4)]


def turned_if(turn, value):
    return jnp.where(turn, value[0].T, value[0]), jnp.where(turn, -value[1].T, value[1])


def start_chain(slabs, pole, *refs):
    near, out, chosen = refs[: slabs // 2], refs[-2], refs[-1]
    me = lax.axis_index("slab")
    distance = me ^ jnp.where(me < slabs // 2, 0, slabs - 1)
    zr, zi, _, _ = scalars_of(pole)
    for k, ref in enumerate(near):

        @pl.when(distance == k)
        def _(ref=ref):
            chosen[...] = ref[...]

    (inverse,) = inverses_of(shifted(unpack(chosen[...]), zr, zi))
    put(out, inverse)


def chain(slabs, me, blocks, links, zr, zi):
    left = me < slabs // 2

    def block(own, j):
        index = jnp.where(left == own, j, slabs - 1 - j)
        return shifted(unpack(blocks[index]), zr, zi)

    def reduced(own, j, inverse):
        from_left = left == own
        k = turned_if(jnp.logical_not(from_left), get(links, jnp.where(from_left, j, slabs - j)))
        out, back = times(inverse, k), adjoint(k)
        return times(back, out), out, back

    return block, reduced


def fill_near(me, target, refs):
    for k, ref in enumerate(refs):
        target[me ^ k] = ref[...] if ref.ndim == target.ndim - 1 else ref[0]


def fill_links(me, target, own, halves):
    core = lax.axis_index("sub")
    target[me] = own[0]
    for i, ref in enumerate(halves):
        target[me ^ (1 + i // 2), core if i % 2 == 0 else 1 - core] = ref[...]


def fill_far(me, target, refs):
    middle, core = target.shape[0] // 2, lax.axis_index("sub")
    for i, ref in enumerate(refs):
        mask = middle + i - i % 2 + jnp.where(i % 2 == 0, core, 1 - core)
        target[me ^ mask] = ref[...] if ref.ndim == target.ndim - 1 else ref[0]


def couple(slabs, pole, start, *refs):
    middle = slabs // 2
    block_refs, own, refs = refs[:middle], refs[middle], refs[middle + 1 :]
    halves, refs = refs[: 2 * middle - 2], refs[2 * middle - 2 :]
    pivot, outward, inward, blocks, links = refs
    me = lax.axis_index("slab")
    zr, zi, _, _ = scalars_of(pole)
    fill_near(me, blocks, block_refs)
    fill_links(me, links, own, halves)
    block, reduced = chain(slabs, me, blocks, links, zr, zi)
    inverse = get(start)
    taken, out, back = reduced(True, 1, inverse)
    put(pivot, minus(block(True, 1), taken))
    put(outward, out)
    put(inward, times(back, inverse))


def advance(slabs, pole, pivot, *refs):
    middle = slabs // 2
    block_refs, (here, there, blocks) = refs[:middle], refs[middle:]
    me = lax.axis_index("slab")
    zr, zi, _, _ = scalars_of(pole)
    fill_far(me, blocks, block_refs)
    block, _ = chain(slabs, me, blocks, None, zr, zi)
    swept = invert([to_tiles(get(pivot)), to_tiles(block(False, 0))], end=SPLIT)
    for ref, tiles in zip((here, there), swept):
        put(ref, from_tiles(tiles))


def advance_on(here, there, own, other):
    swept = invert([to_tiles(get(here)), to_tiles(get(there))], begin=SPLIT)
    for ref, tiles in zip((own, other), swept):
        put(ref, from_tiles(tiles))


def finish(slabs, poles, pole, start, second, end, outward_1, inward_1, *refs):
    middle = slabs // 2
    block_refs, coupling, refs = refs[:slabs], refs[slabs], refs[slabs + 1 :]
    halves, refs = refs[: 2 * middle - 2], refs[2 * middle - 2 :]
    far_refs, refs = refs[:middle], refs[middle:]
    outs, (blocks, links, outward, inward, own, other, work) = refs[:poles], refs[poles:]
    me, mine = lax.axis_index("slab"), lax.axis_index(("pole", "sub"))
    order = start.shape[-1]
    fill_near(me, blocks, block_refs[:middle])
    fill_far(me, blocks, block_refs[middle:])
    fill_links(me, links, coupling, halves)
    fill_far(me, links, far_refs)
    zr, zi, wr, wi = scalars_of(pole)
    block, reduced = chain(slabs, me, blocks, links, zr, zi)
    own[0], own[1], other[0] = start[...], second[...], end[...]
    outward[1], inward[1] = outward_1[...], inward_1[...]

    def other_pivot(j):
        return minus(block(False, j), reduced(False, j, get(other, j - 1))[0])

    def level(j, _):
        inverse = get(own, j - 1)
        taken, out, back = reduced(True, j, inverse)
        one, two = inverses_of(minus(block(True, j), taken), other_pivot(j - 1))
        put(outward, out, j)
        put(inward, times(back, inverse), j)
        put(own, one, j)
        put(other, two, j - 1)
        return 0

    def wider(j, found):
        base, out, back = found
        near_out, near_back = get(outward, j), get(inward, j)
        base = plus(get(own, j - 1), times(times(near_out, base), near_back))
        return base, times(near_out, out), times(back, near_back)

    if middle > 2:
        lax.fori_loop(2, middle, level, 0)
    inverse = get(own, middle - 1)
    taken, out, back = reduced(True, middle, inverse)
    steps = middle - 1 - jnp.where(me < middle, me, slabs - 1 - me)
    pivot = minus(other_pivot(middle - 1), taken)
    if middle == 2:
        made = {}

        def aside(name, make):
            return lambda: made.update({name: make()})

        near_out, near_back = get(outward, 1), get(inward, 1)
        asides = [
            aside("back", lambda: times(back, inverse)),
            aside("half", lambda: times(near_out, inverse)),
            aside("further_out", lambda: times(near_out, out)),
            aside("base", lambda: plus(get(own, 0), times(made["half"], near_back))),
            aside("further_back", lambda: times(made["back"], near_back)),
        ]
        (green,) = inverses_of(pivot, asides=asides)
        found = jax.tree.map(
            lambda new, old: jnp.where(steps > 0, new, old),
            (made["base"], made["further_out"], made["further_back"]),
            (inverse, out, made["back"]),
        )
    else:
        found = inverse, out, times(back, inverse)
        found = lax.fori_loop(0, steps, lambda step, found: wider(middle - 1 - step, found), found)
        (green,) = inverses_of(pivot)
    gr, gi = plus(found[0], times(times(found[1], green), found[2]))
    gr_t, gi_t = gr.T, gi.T
    even, odd = (0.5 * (gr + gr_t), 0.5 * (gi + gi_t)), (0.5 * (gr_t - gr), 0.5 * (gi_t - gi))
    rows = order // poles
    for slot, (ur, ui) in enumerate(((wr, wi), (wr * zr - wi * zi, wr * zi + wi * zr))):
        put(work, (ur * even[1] + ui * even[0], ur * odd[0] - ui * odd[1]), slot)
    for k in range(poles):
        begin = pl.multiple_of((mine ^ k) * rows, rows)
        outs[k][...] = work[:, :, pl.ds(begin, rows), :]


def shards(slabs, poles, onsite, coupling, pole_real, pole_imag, pole_weight):
    order = onsite.shape[-1]
    middle = slabs // 2
    vmem = pl.BlockSpec(memory_space=pltpu.VMEM)
    params = pltpu.CompilerParams(vmem_limit_bytes=40 << 20)
    square_of = jax.ShapeDtypeStruct((order, order), f32)
    complex_of = jax.ShapeDtypeStruct((2, order, order), f32)

    def scratch(*lead):
        return pltpu.VMEM((*lead, order, order), f32)

    def cost(inversions):
        return pl.CostEstimate(
            flops=inversions * 25 * 10**8, bytes_accessed=inversions * 10**6, transcendentals=0
        )

    def swap(value, k):
        return lax.ppermute(value, "slab", [(i, i ^ k) for i in range(slabs)])

    half = pl.pallas_call(
        halve, out_shape=square_of, in_specs=[vmem], out_specs=vmem, compiler_params=params
    )(coupling)
    near_links = [swap(half, k) for k in range(1, middle)]
    packed = pl.pallas_call(
        prepare, out_shape=square_of, in_specs=[vmem], out_specs=vmem, compiler_params=params
    )(onsite)
    pole = pl.pallas_call(
        spread_scalars,
        out_shape=jax.ShapeDtypeStruct((ROWS, order), f32),
        in_specs=[vmem] * 3,
        out_specs=vmem,
        compiler_params=params,
    )(pole_real, pole_imag, pole_weight)

    def far_swap(value, k):
        pairs = [(2 * i + c, 2 * (i ^ (k + c)) + c) for i in range(slabs) for c in range(2)]
        return lax.ppermute(value, ("slab", "sub"), pairs)

    near_blocks = [packed] + [swap(packed, k) for k in range(1, middle)]
    far_blocks = [far_swap(packed, k) for k in range(middle, slabs, 2)]
    far_links = [far_swap(coupling, k) for k in range(middle, slabs, 2)]
    start = pl.pallas_call(
        functools.partial(start_chain, slabs),
        out_shape=complex_of,
        in_specs=[vmem] * (1 + middle),
        out_specs=vmem,
        scratch_shapes=[scratch()],
        compiler_params=params,
        cost_estimate=cost(2),
    )(pole, *near_blocks)

    def both(values, after):
        pairs = []
        for value in values:
            mine, _ = lax.optimization_barrier((value, after))
            pairs += [value, lax.ppermute(mine, "sub", [(0, 1), (1, 0)])]
        return pairs

    arrived = near_links[0]
    near_links = both(near_links, start)
    after = lax.optimization_barrier((start, arrived))[0]
    far_blocks = both(far_blocks, after)
    pivot, *factors = pl.pallas_call(
        functools.partial(couple, slabs),
        out_shape=[complex_of] * 3,
        in_specs=[vmem] * (1 + 3 * middle),
        out_specs=[vmem] * 3,
        scratch_shapes=[scratch(slabs), scratch(slabs, 2)],
        compiler_params=params,
        cost_estimate=pl.CostEstimate(flops=1000, bytes_accessed=1000, transcendentals=0),
    )(pole, start, *near_blocks, coupling, *near_links)
    swept = pl.pallas_call(
        functools.partial(advance, slabs),
        out_shape=[complex_of] * 2,
        in_specs=[vmem] * (2 + middle),
        out_specs=[vmem] * 2,
        scratch_shapes=[scratch(slabs)],
        compiler_params=params,
        cost_estimate=pl.CostEstimate(flops=1000, bytes_accessed=1000, transcendentals=0),
    )(pole, pivot, *far_blocks)
    far_links = both(far_links, swept[0])
    second = pl.pallas_call(
        advance_on,
        out_shape=[complex_of] * 2,
        in_specs=[vmem] * 2,
        out_specs=[vmem] * 2,
        compiler_params=params,
        cost_estimate=cost(2),
    )(*swept)
    blocks, links = near_blocks + far_blocks, [coupling] + near_links + far_links
    pieces = pl.pallas_call(
        functools.partial(finish, slabs, poles),
        out_shape=[jax.ShapeDtypeStruct((2, 2, order // poles, order), f32)] * poles,
        in_specs=[vmem] * (5 + 2 * slabs + middle),
        out_specs=[vmem] * poles,
        scratch_shapes=[
            scratch(slabs),
            scratch(slabs, 2),
            scratch(middle + 1, 2),
            scratch(middle + 1, 2),
            scratch(middle, 2),
            scratch(middle, 2),
            scratch(2, 2),
        ],
        compiler_params=params,
        cost_estimate=cost(2),
    )(pole, start, *second, *factors, *blocks, *links)
    total = pieces[0]
    for k in range(1, poles):
        total = total + lax.ppermute(pieces[k], ("pole", "sub"), [(i, i ^ k) for i in range(poles)])
    return total[0][None], total[1][None]


def solution(mesh):
    in_specs = (
        P(("groups", "slab"), None, None, None),
        P(("groups", "slab"), None, None, None),
        P(("pole", "sub")),
        P(("pole", "sub")),
        P(("pole", "sub"), None),
    )
    out_specs = (
        P(("groups", "slab"), None, ("pole", "sub"), None),
        P(("groups", "slab"), None, ("pole", "sub"), None),
    )
    body = functools.partial(shards, mesh.shape["slab"], mesh.shape["pole"] * mesh.shape["sub"])
    return jax.shard_map(body, mesh=mesh, in_specs=in_specs, out_specs=out_specs, check_vma=False)
```

```python
import functools

import jax
import jax.numpy as jnp
from jax import lax
from jax.experimental import pallas as pl
from jax.experimental.pallas import tpu as pltpu
from jax.sharding import PartitionSpec as P

ROWS = 8
PANEL = 2 * ROWS
SPLIT = 1
f32, bf16 = jnp.float32, jnp.bfloat16
PARTS = ((0, 0), (1, 0), (0, 1), (1, 1), (0, 2), (2, 0))


def row_of(tile, k):
    return jnp.broadcast_to(tile[k : k + 1, :], tile.shape)


def lane_of(tile, k):
    where = jnp.full(tile.shape, k, jnp.int32)
    return jnp.take_along_axis(tile, where, axis=1, mode="promise_in_bounds")


def plus(a, b):
    return a[0] + b[0], a[1] + b[1]


def minus(a, b):
    return a[0] - b[0], a[1] - b[1]


def complex_times(a, b):
    return a[0] * b[0] - a[1] * b[1], a[0] * b[1] + a[1] * b[0]


def sweep_double(tiles, columns, first, lane, subl):
    tiles = list(tiles)
    columns = [list(cols) for cols in columns]
    for k in range(0, ROWS, 2):
        for s, cols in enumerate(columns):

            def entries(pair):
                return [(row_of(pair[0], i), row_of(pair[1], i)) for i in (k, k + 1)]

            (a, c), (b, d) = entries(cols[k]), entries(cols[k + 1])
            det = minus(complex_times(a, d), complex_times(b, c))
            scale = 1.0 / (det[0] * det[0] + det[1] * det[1])
            over = det[0] * scale, -det[1] * scale
            one = cols[k][0] - (subl == k).astype(f32), cols[k][1]
            two = cols[k + 1][0] - (subl == k + 1).astype(f32), cols[k + 1][1]
            one, two = (
                minus(complex_times(one, d), complex_times(two, c)),
                minus(complex_times(two, a), complex_times(one, b)),
            )
            for j in range(k + 2, min(k + 3, ROWS)):
                upper, lower = entries(cols[j])
                taken = plus(complex_times(one, upper), complex_times(two, lower))
                cols[j] = minus(cols[j], complex_times(taken, over))
            one, two = complex_times(one, over), complex_times(two, over)
            for j in range(k + 3, ROWS):
                upper, lower = entries(cols[j])
                cols[j] = minus(cols[j], plus(complex_times(one, upper), complex_times(two, lower)))
            upper, lower = entries(tiles[s])
            upper = upper[0] + (lane == first + k).astype(f32), upper[1]
            lower = lower[0] + (lane == first + k + 1).astype(f32), lower[1]
            tiles[s] = minus(tiles[s], plus(complex_times(one, upper), complex_times(two, lower)))
    return tiles


def sweep_single(tiles, columns, first, lane, subl):
    tiles = list(tiles)
    columns = [list(cols) for cols in columns]
    for k in range(ROWS):
        in_row, in_lane = (subl == k).astype(f32), (lane == first + k).astype(f32)
        for s, cols in enumerate(columns):
            xr, xi = tiles[s]
            tr, ti = cols[k]
            dr, di = row_of(tr, k), row_of(ti, k)
            scale = 1.0 / (dr * dr + di * di)
            rr, ri = dr * scale, -di * scale
            cr = tr - in_row
            cr, ci = cr * rr - ti * ri, cr * ri + ti * rr
            for j in range(k + 1, ROWS):
                ar, ai = row_of(cols[j][0], k), row_of(cols[j][1], k)
                cols[j] = (cols[j][0] - (cr * ar - ci * ai), cols[j][1] - (cr * ai + ci * ar))
            ar, ai = row_of(xr, k) + in_lane, row_of(xi, k)
            tiles[s] = (xr - (cr * ar - ci * ai), xi - (cr * ai + ci * ar))
    return tiles


def spread(tiles, first):
    return [
        [(lane_of(xr, first + k), lane_of(xi, first + k)) for k in range(ROWS)] for xr, xi in tiles
    ]


def follow(tile, columns, swept, inside):
    nr, ni = jnp.where(inside, 0.0, tile[0]), jnp.where(inside, 0.0, tile[1])
    pr = pi = None
    for k, column in enumerate(columns):
        tr, ti = complex_times(column, (row_of(swept[0], k), row_of(swept[1], k)))
        if k % 2 == 0:
            nr, ni = nr - tr, ni - ti
        else:
            pr, pi = (tr, ti) if pr is None else (pr + tr, pi + ti)
    return nr - pr, ni - pi


def follow_all(tiles, columns, swept, inside, after=None):
    if after is None or len(tiles) > 1:
        masks = [inside] * len(tiles)
    else:
        masks = [inside & (tile[1] == tile[1]) for tile in after]
    return [follow(*args) for args in zip(tiles, columns, swept, masks)]


def split(x):
    parts = [x.astype(bf16)]
    for _ in range(2):
        x = x - parts[-1].astype(f32)
        parts.append(x.astype(bf16))
    return parts


def multiply(left, right, columns):
    rows = left[0][0].shape[0]
    lhs = jnp.concatenate(
        [jnp.concatenate((left[0][a], left[1][a]), axis=0) for a, _ in PARTS], axis=1
    )
    rhs = jnp.concatenate(
        [jnp.concatenate((right[0][b], right[1][b]), axis=1) for _, b in PARTS], axis=0
    )
    whole = lax.dot_general(lhs, rhs, (((1,), (0,)), ((), ())), preferred_element_type=f32)
    return (
        whole[:rows, :columns] - whole[rows:, columns:],
        whole[:rows, columns:] + whole[rows:, :columns],
    )


def times(left, right):
    columns = right[0].shape[1]
    return multiply([split(part) for part in left], [split(part) for part in right], columns)


def others_follow(tiles, panel, place):
    order = tiles[0][0].shape[1]

    def padded(rows):
        above, below = PANEL * place, order - PANEL * (place + 1)
        parts = [jnp.zeros((above, order), bf16)] if above else []
        parts += [rows]
        parts += [jnp.zeros((below, order), bf16)] if below else []
        return jnp.concatenate(parts, axis=0)

    left = [split(jnp.concatenate(part, axis=0)) for part in zip(*tiles)]
    right = [[padded(rows) for rows in split(jnp.concatenate(part, axis=0))] for part in zip(*panel)]
    real, imag = multiply(left, right, order)
    return [(real[ROWS * t : ROWS * t + ROWS], imag[ROWS * t : ROWS * t + ROWS]) for t in range(len(tiles))]


def invert(systems, asides=(), begin=0, end=None):
    order = systems[0][0][0].shape[1]
    count, panels = order // ROWS, order // PANEL
    lane = lax.broadcasted_iota(jnp.int32, (ROWS, order), 1)
    subl = lax.broadcasted_iota(jnp.int32, (ROWS, order), 0)
    systems = [list(tiles) for tiles in systems]
    sweep = sweep_double if len(systems) == 1 else sweep_single
    for place in range(panels)[begin:end]:
        a, b = 2 * place, 2 * place + 1
        in_a = (lane >= ROWS * a) & (lane < ROWS * a + ROWS)
        in_b = (lane >= ROWS * b) & (lane < ROWS * b + ROWS)
        soon = [] if place == panels - 1 else [b + 1, b + 2]
        nexts = [[tiles[i] for tiles in systems] for i in soon]
        second = [tiles[b] for tiles in systems]
        if place == begin:
            columns = spread([tiles[a] for tiles in systems], ROWS * a)
        second_columns = spread(second, ROWS * a)
        next_columns = [spread(tiles, ROWS * a) for tiles in nexts]
        first = sweep([tiles[a] for tiles in systems], columns, ROWS * a, lane, subl)
        second = follow_all(second, second_columns, first, in_a)
        columns = spread(second, ROWS * b)
        nexts = [follow_all(tiles, cols, first, in_a, second) for tiles, cols in zip(nexts, next_columns)]
        next_columns = [spread(tiles, ROWS * b) for tiles in nexts]
        first_columns = spread(first, ROWS * b)
        second = sweep(second, columns, ROWS * b, lane, subl)
        for i, cols in enumerate(next_columns):
            nexts[i] = follow_all(nexts[i], cols, second, in_b, nexts[0] if i else None)
            if i == 0:
                columns = spread(nexts[0], ROWS * (b + 1))
        first = follow_all(first, first_columns, second, in_b, nexts[0] if nexts else None)
        rest = [i for i in range(count) if i not in (a, b, *soon)]
        rest.sort(key=lambda i: (i - b) % count)
        for s, tiles in enumerate(systems):
            delta = others_follow([tiles[i] for i in rest], [first[s], second[s]], place)
            for (dr, di), i in zip(delta, rest):
                tiles[i] = (
                    jnp.where(in_a | in_b, 0.0, tiles[i][0]) - dr,
                    jnp.where(in_a | in_b, 0.0, tiles[i][1]) - di,
                )
            tiles[a], tiles[b] = first[s], second[s]
            for i, tile in zip(soon, nexts):
                tiles[i] = tile[s]
        if place < len(asides):
            asides[place]()
    return systems


def to_tiles(value):
    count = value[0].shape[0] // ROWS
    return [tuple(part[ROWS * i : ROWS * i + ROWS] for part in value) for i in range(count)]


def from_tiles(tiles):
    return tuple(jnp.concatenate(part, axis=0) for part in zip(*tiles))


def inverses_of(*values, asides=()):
    return [from_tiles(tiles) for tiles in invert([to_tiles(value) for value in values], asides)]


def adjoint(a):
    return a[0].T, -a[1].T


def get(ref, *index):
    return ref[(*index, 0)], ref[(*index, 1)]


def put(ref, value, *index):
    ref[(*index, 0)], ref[(*index, 1)] = value


def square(order):
    rows = lax.broadcasted_iota(jnp.int32, (order, order), 0)
    columns = lax.broadcasted_iota(jnp.int32, (order, order), 1)
    return rows, columns


def hermitian(onsite):
    return 0.5 * (onsite[0] + onsite[0].T), 0.5 * (onsite[1] - onsite[1].T)


def pack(block):
    rows, columns = square(block[0].shape[0])
    return jnp.where(rows <= columns, *block)


def unpack(packed):
    rows, columns = square(packed.shape[0])
    turned = packed.T
    imag = jnp.where(rows > columns, packed, jnp.where(rows < columns, -turned, 0.0))
    return jnp.where(rows <= columns, packed, turned), imag


def shifted(block, zr, zi):
    rows, columns = square(block[0].shape[0])
    return jnp.where(rows == columns, block[0] - zr, block[0]), jnp.where(rows == columns, -zi, block[1])


def prepare(onsite, packed):
    packed[...] = pack(hermitian(get(onsite, 0)))


def spread_scalars(pole_real, pole_imag, pole_weight, pole):
    width = pole.shape[1]
    pole[0:1, :] = jnp.broadcast_to(pole_real[...].reshape(1, 1), (1, width))
    pole[1:2, :] = jnp.broadcast_to(pole_imag[...].reshape(1, 1), (1, width))
    pole[2:3, :] = jnp.broadcast_to(pole_weight[:, 0:1], (1, width))
    pole[3:4, :] = jnp.broadcast_to(pole_weight[:, 1:2], (1, width))


def halve(coupling, half):
    half[...] = coupling[0, lax.axis_index("sub")]


def scalars_of(pole):
    return [pole[row : row + 1, :] for row in range(4)]


def turned_if(turn, value):
    return jnp.where(turn, value[0].T, value[0]), jnp.where(turn, -value[1].T, value[1])


def start_chain(slabs, pole, *refs):
    near, out, chosen = refs[: slabs // 2], refs[-2], refs[-1]
    me = lax.axis_index("slab")
    distance = me ^ jnp.where(me < slabs // 2, 0, slabs - 1)
    zr, zi, _, _ = scalars_of(pole)
    for k, ref in enumerate(near):

        @pl.when(distance == k)
        def _(ref=ref):
            chosen[...] = ref[...]

    (inverse,) = inverses_of(shifted(unpack(chosen[...]), zr, zi))
    put(out, inverse)


def chain(slabs, me, blocks, links, zr, zi):
    left = me < slabs // 2

    def block(own, j):
        index = jnp.where(left == own, j, slabs - 1 - j)
        return shifted(unpack(blocks[index]), zr, zi)

    def reduced(own, j, inverse):
        from_left = left == own
        k = turned_if(jnp.logical_not(from_left), get(links, jnp.where(from_left, j, slabs - j)))
        out, back = times(inverse, k), adjoint(k)
        return times(back, out), out, back

    return block, reduced


def fill_near(me, target, refs):
    for k, ref in enumerate(refs):
        target[me ^ k] = ref[...] if ref.ndim == target.ndim - 1 else ref[0]


def fill_links(me, target, own, halves):
    core = lax.axis_index("sub")
    target[me] = own[0]
    for i, ref in enumerate(halves):
        target[me ^ (1 + i // 2), core if i % 2 == 0 else 1 - core] = ref[...]


def fill_far(me, target, refs):
    middle, core = target.shape[0] // 2, lax.axis_index("sub")
    for i, ref in enumerate(refs):
        mask = middle + i - i % 2 + jnp.where(i % 2 == 0, core, 1 - core)
        target[me ^ mask] = ref[...] if ref.ndim == target.ndim - 1 else ref[0]


def couple(slabs, pole, start, *refs):
    middle = slabs // 2
    block_refs, own, refs = refs[:middle], refs[middle], refs[middle + 1 :]
    halves, refs = refs[: 2 * middle - 2], refs[2 * middle - 2 :]
    pivot, outward, inward, blocks, links = refs
    me = lax.axis_index("slab")
    zr, zi, _, _ = scalars_of(pole)
    fill_near(me, blocks, block_refs)
    fill_links(me, links, own, halves)
    block, reduced = chain(slabs, me, blocks, links, zr, zi)
    inverse = get(start)
    taken, out, back = reduced(True, 1, inverse)
    put(pivot, minus(block(True, 1), taken))
    put(outward, out)
    put(inward, times(back, inverse))


def advance(slabs, pole, pivot, *refs):
    middle = slabs // 2
    block_refs, (here, there, blocks) = refs[:middle], refs[middle:]
    me = lax.axis_index("slab")
    zr, zi, _, _ = scalars_of(pole)
    fill_far(me, blocks, block_refs)
    block, _ = chain(slabs, me, blocks, None, zr, zi)
    swept = invert([to_tiles(get(pivot)), to_tiles(block(False, 0))], end=SPLIT)
    for ref, tiles in zip((here, there), swept):
        put(ref, from_tiles(tiles))


def advance_on(here, there, own, other):
    swept = invert([to_tiles(get(here)), to_tiles(get(there))], begin=SPLIT)
    for ref, tiles in zip((own, other), swept):
        put(ref, from_tiles(tiles))


def finish(slabs, poles, pole, start, second, end, outward_1, inward_1, *refs):
    middle = slabs // 2
    block_refs, coupling, refs = refs[:slabs], refs[slabs], refs[slabs + 1 :]
    halves, refs = refs[: 2 * middle - 2], refs[2 * middle - 2 :]
    far_refs, refs = refs[:middle], refs[middle:]
    outs, (blocks, links, outward, inward, own, other, work) = refs[:poles], refs[poles:]
    me, mine = lax.axis_index("slab"), lax.axis_index(("pole", "sub"))
    order = start.shape[-1]
    fill_near(me, blocks, block_refs[:middle])
    fill_far(me, blocks, block_refs[middle:])
    fill_links(me, links, coupling, halves)
    fill_far(me, links, far_refs)
    zr, zi, wr, wi = scalars_of(pole)
    block, reduced = chain(slabs, me, blocks, links, zr, zi)
    own[0], own[1], other[0] = start[...], second[...], end[...]
    outward[1], inward[1] = outward_1[...], inward_1[...]

    def other_pivot(j):
        return minus(block(False, j), reduced(False, j, get(other, j - 1))[0])

    def level(j, _):
        inverse = get(own, j - 1)
        taken, out, back = reduced(True, j, inverse)
        one, two = inverses_of(minus(block(True, j), taken), other_pivot(j - 1))
        put(outward, out, j)
        put(inward, times(back, inverse), j)
        put(own, one, j)
        put(other, two, j - 1)
        return 0

    def wider(j, found):
        base, out, back = found
        near_out, near_back = get(outward, j), get(inward, j)
        base = plus(get(own, j - 1), times(times(near_out, base), near_back))
        return base, times(near_out, out), times(back, near_back)

    if middle > 2:
        lax.fori_loop(2, middle, level, 0)
    inverse = get(own, middle - 1)
    taken, out, back = reduced(True, middle, inverse)
    steps = middle - 1 - jnp.where(me < middle, me, slabs - 1 - me)
    pivot = minus(other_pivot(middle - 1), taken)
    if middle == 2:
        made = {}

        def aside(name, make):
            return lambda: made.update({name: make()})

        near_out, near_back = get(outward, 1), get(inward, 1)
        asides = [
            aside("back", lambda: times(back, inverse)),
            aside("half", lambda: times(near_out, inverse)),
            aside("further_out", lambda: times(near_out, out)),
            aside("base", lambda: plus(get(own, 0), times(made["half"], near_back))),
            aside("further_back", lambda: times(made["back"], near_back)),
        ]
        (green,) = inverses_of(pivot, asides=asides)
        found = jax.tree.map(
            lambda new, old: jnp.where(steps > 0, new, old),
            (made["base"], made["further_out"], made["further_back"]),
            (inverse, out, made["back"]),
        )
    else:
        found = inverse, out, times(back, inverse)
        found = lax.fori_loop(0, steps, lambda step, found: wider(middle - 1 - step, found), found)
        (green,) = inverses_of(pivot)
    gr, gi = plus(found[0], times(times(found[1], green), found[2]))
    gr_t, gi_t = gr.T, gi.T
    even, odd = (0.5 * (gr + gr_t), 0.5 * (gi + gi_t)), (0.5 * (gr_t - gr), 0.5 * (gi_t - gi))
    rows = order // poles
    for slot, (ur, ui) in enumerate(((wr, wi), (wr * zr - wi * zi, wr * zi + wi * zr))):
        put(work, (ur * even[1] + ui * even[0], ur * odd[0] - ui * odd[1]), slot)
    for k in range(poles):
        begin = pl.multiple_of((mine ^ k) * rows, rows)
        outs[k][...] = work[:, :, pl.ds(begin, rows), :]


def shards(slabs, poles, onsite, coupling, pole_real, pole_imag, pole_weight):
    order = onsite.shape[-1]
    middle = slabs // 2
    vmem = pl.BlockSpec(memory_space=pltpu.VMEM)
    params = pltpu.CompilerParams(vmem_limit_bytes=40 << 20)
    square_of = jax.ShapeDtypeStruct((order, order), f32)
    complex_of = jax.ShapeDtypeStruct((2, order, order), f32)

    def scratch(*lead):
        return pltpu.VMEM((*lead, order, order), f32)

    def cost(inversions):
        return pl.CostEstimate(
            flops=inversions * 25 * 10**8, bytes_accessed=inversions * 10**6, transcendentals=0
        )

    def swap(value, k):
        return lax.ppermute(value, "slab", [(i, i ^ k) for i in range(slabs)])

    half = pl.pallas_call(
        halve, out_shape=square_of, in_specs=[vmem], out_specs=vmem, compiler_params=params
    )(coupling)
    near_links = [swap(half, k) for k in range(1, middle)]
    packed = pl.pallas_call(
        prepare, out_shape=square_of, in_specs=[vmem], out_specs=vmem, compiler_params=params
    )(onsite)
    pole = pl.pallas_call(
        spread_scalars,
        out_shape=jax.ShapeDtypeStruct((ROWS, order), f32),
        in_specs=[vmem] * 3,
        out_specs=vmem,
        compiler_params=params,
    )(pole_real, pole_imag, pole_weight)

    def far_swap(value, k):
        pairs = [(2 * i + c, 2 * (i ^ (k + c)) + c) for i in range(slabs) for c in range(2)]
        return lax.ppermute(value, ("slab", "sub"), pairs)

    near_blocks = [packed] + [swap(packed, k) for k in range(1, middle)]
    far_blocks = [far_swap(packed, k) for k in range(middle, slabs, 2)]
    far_links = [far_swap(coupling, k) for k in range(middle, slabs, 2)]
    start = pl.pallas_call(
        functools.partial(start_chain, slabs),
        out_shape=complex_of,
        in_specs=[vmem] * (1 + middle),
        out_specs=vmem,
        scratch_shapes=[scratch()],
        compiler_params=params,
        cost_estimate=cost(2),
    )(pole, *near_blocks)

    def both(values, after):
        pairs = []
        for value in values:
            mine, _ = lax.optimization_barrier((value, after))
            pairs += [value, lax.ppermute(mine, "sub", [(0, 1), (1, 0)])]
        return pairs

    arrived = near_links[0]
    near_links = both(near_links, start)
    after = lax.optimization_barrier((start, arrived))[0]
    far_blocks = both(far_blocks, after)
    pivot, *factors = pl.pallas_call(
        functools.partial(couple, slabs),
        out_shape=[complex_of] * 3,
        in_specs=[vmem] * (1 + 3 * middle),
        out_specs=[vmem] * 3,
        scratch_shapes=[scratch(slabs), scratch(slabs, 2)],
        compiler_params=params,
        cost_estimate=pl.CostEstimate(flops=1000, bytes_accessed=1000, transcendentals=0),
    )(pole, start, *near_blocks, coupling, *near_links)
    swept = pl.pallas_call(
        functools.partial(advance, slabs),
        out_shape=[complex_of] * 2,
        in_specs=[vmem] * (2 + middle),
        out_specs=[vmem] * 2,
        scratch_shapes=[scratch(slabs)],
        compiler_params=params,
        cost_estimate=pl.CostEstimate(flops=1000, bytes_accessed=1000, transcendentals=0),
    )(pole, pivot, *far_blocks)
    far_links = both(far_links, swept[0])
    second = pl.pallas_call(
        advance_on,
        out_shape=[complex_of] * 2,
        in_specs=[vmem] * 2,
        out_specs=[vmem] * 2,
        compiler_params=params,
        cost_estimate=cost(2),
    )(*swept)
    blocks, links = near_blocks + far_blocks, [coupling] + near_links + far_links
    pieces = pl.pallas_call(
        functools.partial(finish, slabs, poles),
        out_shape=[jax.ShapeDtypeStruct((2, 2, order // poles, order), f32)] * poles,
        in_specs=[vmem] * (5 + 2 * slabs + middle),
        out_specs=[vmem] * poles,
        scratch_shapes=[
            scratch(slabs),
            scratch(slabs, 2),
            scratch(middle + 1, 2),
            scratch(middle + 1, 2),
            scratch(middle, 2),
            scratch(middle, 2),
            scratch(2, 2),
        ],
        compiler_params=params,
        cost_estimate=cost(2),
    )(pole, start, *second, *factors, *blocks, *links)
    total = pieces[0]
    for k in range(1, poles):
        total = total + lax.ppermute(pieces[k], ("pole", "sub"), [(i, i ^ k) for i in range(poles)])
    return total[0][None], total[1][None]


def solution(mesh):
    in_specs = (
        P(("groups", "slab"), None, None, None),
        P(("groups", "slab"), None, None, None),
        P(("pole", "sub")),
        P(("pole", "sub")),
        P(("pole", "sub"), None),
    )
    out_specs = (
        P(("groups", "slab"), None, ("pole", "sub"), None),
        P(("groups", "slab"), None, ("pole", "sub"), None),
    )
    body = functools.partial(shards, mesh.shape["slab"], mesh.shape["pole"] * mesh.shape["sub"])
    return jax.shard_map(body, mesh=mesh, in_specs=in_specs, out_specs=out_specs, check_vma=False)
```
